512 devices in a mesh: pb: 16 (over z, x_hi), ka: 32 (over x_lo, y, core).
Axes of the slice: x: 4 (x_hi: 2, x_lo: 2; x = x_hi * 2 + x_lo), y: 8, z: 8, core: 2. Of those that a mesh axis runs over, the one named last changes fastest.
Arguments:
- queries: float32 [4096, 256], P(('ka', 'pb')), may hold values from -5 to 5
- key_pair: float32 [32768, 256], P(('pb', 'ka')), may hold values from -5 to 5
- values: float32 [32768, 256], P(('pb', 'ka')), may hold values from -6 to 6
- grad_out: float32 [4096, 256], P(('ka', 'pb')), may hold values from -6 to 6
Outputs:
- attended: float32 [4096, 256], P(('ka', 'pb'))
- grad_queries: float32 [4096, 256], P(('ka', 'pb'))
- grad_keys: float32 [32768, 256], P(('pb', 'ka'))
- grad_values: float32 [32768, 256], P(('pb', 'ka'))
The draws below stay inside these ranges and needn't reach their ends.
All inputs are finite; a program needn't handle non-finite values.
Results may differ from the reference program's by a relative error of at most 0.0003.
Values sent between devices are 32-bit elements; how exact they have to be, the bound alone decides.
No kernel may reach another device: no remote copies, remote signals or barrier semaphores. Data moves between devices by JAX's collectives and lax.ppermute only.
A program may use at most 64 MiB of HBM per device.

```python
import jax
import jax.numpy as jnp
from jax import lax

HQ = 128
HV = 256
NQ = 4096
NK = 32768


def draw_queries(key, part):
    key = jax.random.fold_in(key, 1)
    return jnp.clip(jax.random.normal(key, (NQ, 2 * HQ), jnp.float32), -5.0, 5.0)


def draw_key_pair(key, part):
    key = jax.random.fold_in(key, 2)
    return jnp.clip(jax.random.normal(key, (NK, 2 * HQ), jnp.float32), -5.0, 5.0)


def block_levels(rng, shape, split, low, high):
    gain, own = 1.0, jax.random.fold_in(rng, 6)
    for dim, parts in split:
        heights = jnp.exp(jax.random.uniform(jax.random.fold_in(own, dim), (parts,), jnp.float32, low / len(split), high / len(split)))
        gain = gain * jnp.repeat(heights, shape[dim] // parts).reshape([-1 if axis == dim else 1 for axis in range(len(shape))])
    return gain


def scatter_about(rng, shape, deviation, most, split=(), kind=jnp.bfloat16):
    values = deviation * jax.random.normal(rng, shape, jnp.float32)
    if split:
        values = values * block_levels(rng, shape, split, -0.22, 0.18)
    return jnp.clip(values, -most, most).astype(kind)


def setup_inputs(seed: int = 0) -> dict:
    arg_keys = jax.random.split(jax.random.key(seed), 5)
    return {
        "queries": draw_queries(jax.random.fold_in(arg_keys[4], 71), 0),
        "key_pair": draw_key_pair(jax.random.fold_in(arg_keys[4], 71), 0),
        "values": scatter_about(arg_keys[2], (NK, HV), 1.0, 6.0, ((0, 512),), jnp.float32),
        "grad_out": scatter_about(arg_keys[3], (NQ, HV), 1.0, 6.0, ((0, 512),), jnp.float32),
    }


LAMBDA = 0.5


def reference(queries, key_pair, values, grad_out):
    hp = lax.Precision.HIGHEST
    scale = HQ ** -0.5
    rows_blk = min(NQ, 512)
    count_blk = NQ // rows_blk
    first_k = key_pair[:, :HQ]
    second_k = key_pair[:, HQ:]
    q_blocks = queries.reshape(count_blk, rows_blk, 2 * HQ)
    g_blocks = grad_out.reshape(count_blk, rows_blk, HV)

    def step(carry, inputs):
        key_acc, value_acc = carry
        q_blk, g_blk = inputs
        first_q = q_blk[:, :HQ]
        second_q = q_blk[:, HQ:]
        score_one = jnp.dot(first_q, first_k.T, precision=hp, preferred_element_type=jnp.float32) * scale
        score_two = jnp.dot(second_q, second_k.T, precision=hp, preferred_element_type=jnp.float32) * scale
        prob_one = jax.nn.softmax(score_one, axis=1)
        prob_two = jax.nn.softmax(score_two, axis=1)
        attend_one = jnp.dot(prob_one, values, precision=hp, preferred_element_type=jnp.float32)
        attend_two = jnp.dot(prob_two, values, precision=hp, preferred_element_type=jnp.float32)
        result = attend_one - LAMBDA * attend_two
        grad_prob = jnp.dot(g_blk, values.T, precision=hp, preferred_element_type=jnp.float32)
        delta_one = jnp.sum(g_blk * attend_one, axis=1, keepdims=True)
        delta_two = jnp.sum(g_blk * attend_two, axis=1, keepdims=True)
        slope_one = prob_one * (grad_prob - delta_one)
        slope_two = -LAMBDA * prob_two * (grad_prob - delta_two)
        grad_q = jnp.concatenate([
            jnp.dot(slope_one, first_k, precision=hp, preferred_element_type=jnp.float32) * scale,
            jnp.dot(slope_two, second_k, precision=hp, preferred_element_type=jnp.float32) * scale], axis=1)
        grad_k = jnp.concatenate([
            jnp.dot(slope_one.T, first_q, precision=hp, preferred_element_type=jnp.float32) * scale,
            jnp.dot(slope_two.T, second_q, precision=hp, preferred_element_type=jnp.float32) * scale], axis=1)
        grad_v = jnp.dot((prob_one - LAMBDA * prob_two).T, g_blk, precision=hp, preferred_element_type=jnp.float32)
        return (key_acc + grad_k, value_acc + grad_v), (result, grad_q)

    start = (jnp.zeros((NK, 2 * HQ), jnp.float32), jnp.zeros((NK, HV), jnp.float32))
    (grad_keys, grad_values), (attended, grad_queries) = lax.scan(step, start, (q_blocks, g_blocks))
    return attended.reshape(NQ, HV), grad_queries.reshape(NQ, 2 * HQ), grad_keys, grad_values
```

```python
import jax
import jax.numpy as jnp
from jax import lax
from jax.sharding import Mesh, PartitionSpec as P

LAMBDA = 0.5
PB = ("z2", "z1", "z0", "xh")
KA = ("xl", "y2", "y1", "y0", "c")
KEY_GROUP = ("xh", "xl", "y0")
QUERY_GROUP = ("z2", "z1", "z0", "y2", "y1")
CORE = "c"


def dot(left, right, dims):
    return lax.dot_general(
        left, right, (dims, ((), ())), precision=lax.Precision.HIGHEST, preferred_element_type=jnp.float32
    )


def swap(x):
    return lax.ppermute(x, CORE, [(0, 1), (1, 0)])


def spread(x, axes, count):
    return lax.all_to_all(jnp.broadcast_to(x[None], (count,) + x.shape), axes, 0, 0, tiled=True)


def per_device(queries, key_pair, values, grad_out):
    half = key_pair.shape[1] // 2
    scale = half ** (-0.5)
    keys_in, queries_in = 8, 32
    kv = jnp.concatenate([key_pair, values], axis=1)
    qg = jnp.concatenate([queries, grad_out], axis=1)
    kv_own = spread(kv, KEY_GROUP, keys_in).reshape(-1, kv.shape[1])
    kv_other = swap(kv_own)
    qg_all = spread(qg, QUERY_GROUP, queries_in).reshape(-1, qg.shape[1])
    kv_all = jnp.concatenate([kv_own, kv_other], axis=0)
    q1, q2, g = qg_all[:, :half] * scale, qg_all[:, half : 2 * half] * scale, qg_all[:, 2 * half :]
    k1, k2, v = kv_all[:, :half], kv_all[:, half : 2 * half], kv_all[:, 2 * half :]
    s1 = dot(k1, q1, ((1,), (1,)))
    s2 = dot(k2, q2, ((1,), (1,)))
    dp = dot(v, g, ((1,), (1,)))
    m1, m2 = jnp.max(s1, axis=0), jnp.max(s2, axis=0)
    w1, w2 = jnp.exp(s1 - m1[None]), jnp.exp(s2 - m2[None])
    stats = jnp.stack(
        [m1, m2, jnp.sum(w1, 0), jnp.sum(w2, 0), jnp.sum(w1 * dp, 0), jnp.sum(w2 * dp, 0), m1, m2]
    )
    every = spread(stats, QUERY_GROUP, queries_in).reshape((queries_in,) + stats.shape)
    top = jnp.max(every[:, :2], axis=0)
    factor = jnp.exp(every[:, :2] - top[None])
    total = jnp.sum(every[:, 2:4] * factor, axis=0)
    delta = jnp.sum(every[:, 4:6] * factor, axis=0) / total
    own = jnp.exp(stats[:2] - top) / total
    p1, p2 = w1 * own[0], w2 * own[1]
    mixed = p1 - LAMBDA * p2
    g1 = p1 * (dp - delta[0])
    g2 = -LAMBDA * p2 * (dp - delta[1])
    dkv = jnp.concatenate(
        [dot(g1, q1, ((1,), (0,))), dot(g2, q2, ((1,), (0,))), dot(mixed, g, ((1,), (0,)))], axis=1
    )
    rows = kv_own.shape[0]
    dkv_own = dkv[:rows] + swap(dkv[rows:])
    dkv_parts = lax.all_to_all(
        dkv_own.reshape(keys_in, -1, dkv.shape[1]), KEY_GROUP, 0, 0, tiled=True
    )
    dkv_sum = jnp.sum(dkv_parts, axis=0)
    dq = jnp.concatenate(
        [dot(mixed, v, ((0,), (0,))), dot(g1, k1, ((0,), (0,))) * scale, dot(g2, k2, ((0,), (0,))) * scale],
        axis=1,
    )
    dq_parts = lax.all_to_all(dq.reshape(queries_in, -1, dq.shape[1]), QUERY_GROUP, 0, 0, tiled=True)
    dq_sum = jnp.sum(dq_parts, axis=0)
    wide = 2 * half
    return dq_sum[:, :wide], dq_sum[:, wide:], dkv_sum[:, :wide], dkv_sum[:, wide:]


def solution(mesh):
    fine = Mesh(mesh.devices.reshape((2,) * 9), PB + KA)
    by_query, by_key = P(KA + PB, None), P(PB + KA, None)
    return jax.shard_map(
        per_device,
        mesh=fine,
        in_specs=(by_query, by_key, by_key, by_query),
        out_specs=(by_query, by_query, by_key, by_key),
        check_vma=False,
    )
```

```python
import jax
import jax.numpy as jnp
from jax import lax
from jax.experimental import pallas as pl
from jax.experimental.pallas import tpu as pltpu
from jax.sharding import Mesh, PartitionSpec as P

LAMBDA = 0.5
PB = ("z2", "z1", "z0", "xh")
KA = ("xl", "y2", "y1", "y0", "c")
KEY_GROUP = ("xh", "xl", "y0")
KEYS_IN = 8
QUERY_GROUP = ("z2", "z1", "z0", "y2", "y1")
QUERIES_IN = 32
CORE = "c"
STRIP = 256
F32, BF16 = jnp.float32, jnp.bfloat16
VMEM_LIMIT = 56 * 1024 * 1024


def call(body, out_shape, flops, moved):
    return pl.pallas_call(
        body,
        out_shape=out_shape,
        cost_estimate=pl.CostEstimate(flops=flops, bytes_accessed=moved, transcendentals=0),
        compiler_params=pltpu.CompilerParams(vmem_limit_bytes=VMEM_LIMIT),
    )


def shape(dtype, *dims):
    return jax.ShapeDtypeStruct(dims, dtype)


def parts(x, count):
    out = []
    for _ in range(count):
        out.append(x.astype(BF16))
        x = x - out[-1].astype(F32)
    return out


def dot(left, right, dims=((1,), (0,))):
    return lax.dot_general(left, right, (dims, ((), ())), preferred_element_type=F32)


def beside(*blocks):
    return jnp.concatenate(blocks, axis=1)


def lay_out(queries_ref, grad_ref, key_ref, value_ref, kv_ref, qg_ref):
    wide = key_ref.shape[1]
    for n in range(kv_ref.shape[0]):
        kv_ref[n, :, :wide] = key_ref[...]
        kv_ref[n, :, wide:] = value_ref[...]
    for n in range(qg_ref.shape[0]):
        qg_ref[n, :, :wide] = queries_ref[...]
        qg_ref[n, :, wide:] = grad_ref[...]


def split_keys(kv_ref, key_ref, value_ref, turned_ref):
    wide = kv_ref.shape[1] // 2
    for n, part in enumerate(parts(kv_ref[:, :wide], 3)):
        key_ref[n] = part
    for n, part in enumerate(parts(kv_ref[:, wide:], 2)):
        value_ref[n] = part
    for n, part in enumerate(parts(kv_ref[...].T, 2)):
        turned_ref[n] = part


def forward(own_key, own_value, other_key, other_value, qg_ref, w1_ref, w2_ref, dp_ref, stats_ref):
    half = qg_ref.shape[1] // 4
    scale = half ** (-0.5)
    g_hi, g_lo = parts(qg_ref[:, 2 * half :], 2)
    query = []
    for first in (0, half):
        hi, mid, low = parts(qg_ref[:, first : first + half] * scale, 3)
        query.append((beside(hi, mid), beside(low, hi)))
    rows = own_key.shape[1]
    tops = [None, None]
    for which, (key_ref, value_ref) in enumerate(((own_key, own_value), (other_key, other_value))):
        for start in range(0, rows, STRIP):
            here = pl.ds(start, STRIP)
            there = pl.ds(which * rows + start, STRIP)
            for head, w_ref in enumerate((w1_ref, w2_ref)):
                cols = pl.ds(head * half, half)
                hi, mid, low = (key_ref[n, here, cols] for n in range(3))
                main, rest = query[head]
                across = ((1,), (1,))
                score = (
                    dot(beside(hi, hi), main, across)
                    + dot(beside(mid, mid), main, across)
                    + dot(beside(hi, low), rest, across)
                )
                w_ref[there, :] = score
                top = jnp.max(score, axis=0, keepdims=True)
                tops[head] = top if tops[head] is None else jnp.maximum(tops[head], top)
            v_hi, v_lo = value_ref[0, here, :], value_ref[1, here, :]
            dp_ref[there, :] = (
                dot(v_hi, g_hi, ((1,), (1,))) + dot(v_hi, g_lo, ((1,), (1,))) + dot(v_lo, g_hi, ((1,), (1,)))
            )
    for head, w_ref in enumerate((w1_ref, w2_ref)):
        mass = jnp.zeros_like(tops[head])
        lean = jnp.zeros_like(tops[head])
        for start in range(0, 2 * rows, STRIP):
            here = pl.ds(start, STRIP)
            weight = jnp.exp(w_ref[here, :] - tops[head])
            w_ref[here, :] = weight
            mass = mass + jnp.sum(weight, axis=0, keepdims=True)
            lean = lean + jnp.sum(weight * dp_ref[here, :], axis=0, keepdims=True)
        stats_ref[head : head + 1, :] = tops[head]
        stats_ref[2 + head : 3 + head, :] = mass
        stats_ref[4 + head : 5 + head, :] = lean
    stats_ref[6:8, :] = jnp.zeros_like(stats_ref[6:8, :])


def key_side(w1_ref, w2_ref, dp_ref, qg_ref, stats_ref, every_ref, own_ref, other_ref, slopes_ref):
    half = qg_ref.shape[1] // 4
    scale = half ** (-0.5)
    every = every_ref[...]
    top = jnp.max(every[:, 0:2, :], axis=0)
    factor = jnp.exp(every[:, 0:2, :] - top[None])
    total = jnp.sum(every[:, 2:4, :] * factor, axis=0)
    delta = jnp.sum(every[:, 4:6, :] * factor, axis=0) / total
    rescale = jnp.exp(stats_ref[0:2, :] - top) / total
    g_hi, g_lo = parts(qg_ref[:, 2 * half :], 2)
    query = [parts(qg_ref[:, first : first + half] * scale, 2) for first in (0, half)]
    rows = own_ref.shape[0]
    for which, out_ref in enumerate((own_ref, other_ref)):
        for start in range(0, rows, STRIP):
            here = pl.ds(start, STRIP)
            there = pl.ds(which * rows + start, STRIP)
            dp = dp_ref[there, :]
            p1 = w1_ref[there, :] * rescale[0:1]
            p2 = w2_ref[there, :] * (-LAMBDA * rescale[1:2])
            slopes = (p1 * (dp - delta[0:1]), p2 * (dp - delta[1:2]))
            mix_hi, mix_lo = parts(p1 + p2, 2)
            slopes_ref[0, there, :] = mix_hi
            slopes_ref[1, there, :] = mix_lo
            for head in range(2):
                hi, lo = parts(slopes[head], 2)
                slopes_ref[2 + 2 * head, there, :] = hi
                slopes_ref[3 + 2 * head, there, :] = lo
                q_hi, q_lo = query[head]
                both = dot(hi, beside(q_hi, q_lo))
                out_ref[here, head * half : (head + 1) * half] = both[:, :half] + both[:, half:] + dot(lo, q_hi)
            out_ref[here, 2 * half :] = dot(mix_hi, g_hi) + dot(mix_hi, g_lo) + dot(mix_lo, g_hi)


def query_side(slopes_ref, own_ref, other_ref, out_ref):
    rows = own_ref.shape[2]
    wide = own_ref.shape[1] // 2
    half = wide // 2
    scale = half ** (-0.5)

    def product(first, count, at):
        total = None
        for which, turned in enumerate((own_ref, other_ref)):
            there = pl.ds(which * rows, rows)
            hi, lo = turned[0, first : first + count, :], turned[1, first : first + count, :]
            s_hi, s_lo = slopes_ref[at, there, :], slopes_ref[at + 1, there, :]
            term = dot(hi, s_hi) + dot(hi, s_lo) + dot(lo, s_hi)
            total = term if total is None else total + term
        return total.T

    out_ref[:, :wide] = product(wide, wide, 0)
    out_ref[:, wide : wide + half] = product(0, half, 2) * scale
    out_ref[:, wide + half :] = product(half, half, 4) * scale


def swap(x):
    return lax.ppermute(x, CORE, [(0, 1), (1, 0)])


def exchange(x, axes):
    return lax.all_to_all(x, axes, 0, 0, tiled=True)


def per_device(queries, key_pair, values, grad_out):
    wide = values.shape[1]
    own_keys, own_rows = key_pair.shape[0], queries.shape[0]
    rows, columns = KEYS_IN * own_keys, QUERIES_IN * own_rows
    kv, qg = call(
        lay_out,
        (shape(F32, KEYS_IN, own_keys, 2 * wide), shape(F32, QUERIES_IN, own_rows, 2 * wide)),
        0,
        4 * 2 * wide * (rows + columns),
    )(queries, grad_out, key_pair, values)
    kv_own = exchange(kv, KEY_GROUP).reshape(rows, 2 * wide)
    kv_other = swap(kv_own)
    qg_all = exchange(qg, QUERY_GROUP).reshape(columns, 2 * wide)
    split = call(
        split_keys,
        (shape(BF16, 3, rows, wide), shape(BF16, 2, rows, wide), shape(BF16, 2, 2 * wide, rows)),
        0,
        4 * 2 * wide * rows * 3,
    )
    own_key, own_value, own_turned = split(kv_own)
    other_key, other_value, other_turned = split(kv_other)
    big = shape(F32, 2 * rows, columns)
    pairs = 2 * rows * columns
    w1, w2, dp, stats = call(
        forward, (big, big, big, shape(F32, 8, columns)), 2 * pairs * wide * 9, 4 * pairs * 3
    )(own_key, own_value, other_key, other_value, qg_all)
    every = exchange(
        jnp.broadcast_to(stats[None], (QUERIES_IN,) + stats.shape), QUERY_GROUP
    ).reshape((QUERIES_IN,) + stats.shape)
    half_grad = shape(F32, rows, 2 * wide)
    dkv_own, dkv_other, slopes = call(
        key_side, (half_grad, half_grad, shape(BF16, 6, 2 * rows, columns)), 2 * pairs * wide * 6, 4 * pairs * 6
    )(w1, w2, dp, qg_all, stats, every)
    moved = swap(dkv_other)
    dq = call(query_side, shape(F32, columns, 2 * wide), 2 * pairs * wide * 6, 4 * pairs * 4)(
        slopes, own_turned, other_turned
    )
    dq_sum = jnp.sum(exchange(dq.reshape(QUERIES_IN, own_rows, 2 * wide), QUERY_GROUP), axis=0)
    dkv = (dkv_own + moved).reshape(KEYS_IN, own_keys, 2 * wide)
    dkv_sum = jnp.sum(exchange(dkv, KEY_GROUP), axis=0)
    return dq_sum[:, :wide], dq_sum[:, wide:], dkv_sum[:, :wide], dkv_sum[:, wide:]


def solution(mesh):
    fine = Mesh(mesh.devices.reshape((2,) * 9), PB + KA)
    by_query, by_key = P(KA + PB, None), P(PB + KA, None)
    return jax.shard_map(
        per_device,
        mesh=fine,
        in_specs=(by_query, by_key, by_key, by_query),
        out_specs=(by_query, by_query, by_key, by_key),
        check_vma=False,
    )
```

```python
import jax
import jax.numpy as jnp
from jax import lax
from jax.experimental import pallas as pl
from jax.experimental.pallas import tpu as pltpu
from jax.sharding import Mesh, PartitionSpec as P

LAMBDA = 0.5
PB = ("z2", "z1", "z0", "xh")
KA = ("xl", "y2", "y1", "y0", "c")
RING = ("xh", "xl")
PAIR = "y0"
AROUND = 4
NEAR = 2
KEYS_IN = NEAR * AROUND
QUERY_GROUP = ("z2", "z1", "z0", "y2", "y1")
QUERIES_IN = 32
CORE = "c"
STRIP = 256
F32, BF16 = jnp.float32, jnp.bfloat16
VMEM_LIMIT = 16 * 1024 * 1024


def call(body, out_shape, flops, moved, **given):
    return pl.pallas_call(
        body,
        out_shape=out_shape,
        cost_estimate=pl.CostEstimate(flops=flops, bytes_accessed=moved, transcendentals=0),
        compiler_params=pltpu.CompilerParams(vmem_limit_bytes=VMEM_LIMIT),
        **given,
    )


def shape(dtype, *dims):
    return jax.ShapeDtypeStruct(dims, dtype)


def parts(x, count):
    out = []
    for _ in range(count):
        out.append(x.astype(BF16))
        x = x - out[-1].astype(F32)
    return out


def dot(left, right, dims=((1,), (0,))):
    return lax.dot_general(left, right, (dims, ((), ())), preferred_element_type=F32)


def beside(*blocks):
    return jnp.concatenate(blocks, axis=1)


def lay_out(left_ref, right_ref, out_ref):
    wide = left_ref.shape[1]
    for n in range(out_ref.shape[0]):
        out_ref[n, :, :wide] = left_ref[...]
        out_ref[n, :, wide:] = right_ref[...]


def lay_once(left_ref, right_ref, out_ref):
    wide = left_ref.shape[1]
    out_ref[:, :wide] = left_ref[...]
    out_ref[:, wide:] = right_ref[...]


def stack(*refs):
    *in_refs, out_ref = refs
    rows = in_refs[0].shape[0]
    for n, ref in enumerate(in_refs):
        out_ref[pl.ds(n * rows, rows), :] = ref[...]


def split_keys(*refs):
    *in_refs, key_ref, value_ref, turned_ref = refs
    rows, wide = in_refs[0].shape[0], in_refs[0].shape[1] // 2
    for at, ref in enumerate(in_refs):
        here = pl.ds(at * rows, rows)
        for n, part in enumerate(parts(ref[:, :wide], 3)):
            key_ref[n, here, :] = part
        for n, part in enumerate(parts(ref[:, wide:], 2)):
            value_ref[n, here, :] = part
        for n, part in enumerate(parts(ref[...].T, 2)):
            turned_ref[n, :, here] = part


def forward(own_key, own_value, other_key, other_value, qg_ref, w1_ref, w2_ref, dp_ref, stats_ref):
    half = qg_ref.shape[1] // 4
    scale = half ** (-0.5)
    g_hi, g_lo = parts(qg_ref[:, 2 * half :], 2)
    query = []
    for first in (0, half):
        hi, mid, low = parts(qg_ref[:, first : first + half] * scale, 3)
        query.append((beside(hi, mid), beside(low, hi)))
    rows = own_key.shape[1]
    tops = [None, None]
    for which, (key_ref, value_ref) in enumerate(((own_key, own_value), (other_key, other_value))):
        for start in range(0, rows, STRIP):
            here = pl.ds(start, STRIP)
            there = pl.ds(which * rows + start, STRIP)
            for head, w_ref in enumerate((w1_ref, w2_ref)):
                cols = pl.ds(head * half, half)
                hi, mid, low = (key_ref[n, here, cols] for n in range(3))
                main, rest = query[head]
                across = ((1,), (1,))
                score = (
                    dot(beside(hi, hi), main, across)
                    + dot(beside(mid, mid), main, across)
                    + dot(beside(hi, low), rest, across)
                )
                w_ref[there, :] = score
                top = jnp.max(score, axis=0, keepdims=True)
                tops[head] = top if tops[head] is None else jnp.maximum(tops[head], top)
            v_hi, v_lo = value_ref[0, here, :], value_ref[1, here, :]
            dp_ref[there, :] = (
                dot(v_hi, g_hi, ((1,), (1,))) + dot(v_hi, g_lo, ((1,), (1,))) + dot(v_lo, g_hi, ((1,), (1,)))
            )
    numbers = []
    columns = qg_ref.shape[0]
    for head, w_ref in enumerate((w1_ref, w2_ref)):
        mass = jnp.zeros_like(tops[head])
        lean = jnp.zeros_like(tops[head])
        for start in range(0, 2 * rows, STRIP):
            here = pl.ds(start, STRIP)
            weight = jnp.exp(w_ref[here, :] - tops[head])
            w_ref[here, :] = weight
            mass = mass + jnp.sum(weight, axis=0, keepdims=True)
            lean = lean + jnp.sum(weight * dp_ref[here, :], axis=0, keepdims=True)
        numbers.append((tops[head], mass, lean))
    blank = jnp.zeros((2, columns), F32)
    stats = jnp.concatenate([pair[n] for n in range(3) for pair in numbers] + [blank], axis=0)
    for n in range(stats_ref.shape[0]):
        stats_ref[n] = stats


def key_side(w1_ref, w2_ref, dp_ref, qg_ref, stats_ref, every_ref, own_ref, other_ref, slopes_ref):
    half = qg_ref.shape[1] // 4
    scale = half ** (-0.5)
    every = every_ref[...]
    top = jnp.max(every[:, 0:2, :], axis=0)
    factor = jnp.exp(every[:, 0:2, :] - top[None])
    total = jnp.sum(every[:, 2:4, :] * factor, axis=0)
    delta = jnp.sum(every[:, 4:6, :] * factor, axis=0) / total
    rescale = jnp.exp(stats_ref[0, 0:2, :] - top) / total
    g_hi, g_lo = parts(qg_ref[:, 2 * half :], 2)
    query = [parts(qg_ref[:, at : at + half] * scale, 2) for at in (0, half)]
    first = 0
    for out_ref in (own_ref, other_ref):
        for start in range(0, out_ref.shape[0], STRIP):
            here = pl.ds(start, STRIP)
            there = pl.ds(first, STRIP)
            first += STRIP
            dp = dp_ref[there, :]
            p1 = w1_ref[there, :] * rescale[0:1]
            p2 = w2_ref[there, :] * (-LAMBDA * rescale[1:2])
            slopes = (p1 * (dp - delta[0:1]), p2 * (dp - delta[1:2]))
            mix_hi, mix_lo = parts(p1 + p2, 2)
            slopes_ref[0, there, :] = mix_hi
            slopes_ref[1, there, :] = mix_lo
            for head in range(2):
                hi, lo = parts(slopes[head], 2)
                slopes_ref[2 + 2 * head, there, :] = hi
                slopes_ref[3 + 2 * head, there, :] = lo
                q_hi, q_lo = query[head]
                both = dot(hi, beside(q_hi, q_lo))
                out_ref[here, head * half : (head + 1) * half] = both[:, :half] + both[:, half:] + dot(lo, q_hi)
            out_ref[here, 2 * half :] = dot(mix_hi, g_hi) + dot(mix_hi, g_lo) + dot(mix_lo, g_hi)


def query_side(slopes_ref, own_ref, other_ref, out_ref):
    rows = own_ref.shape[2]
    wide = own_ref.shape[1] // 2
    half = wide // 2
    scale = half ** (-0.5)

    def product(first, count, at):
        total = None
        for which, turned in enumerate((own_ref, other_ref)):
            there = pl.ds(which * rows, rows)
            hi, lo = turned[0, first : first + count, :], turned[1, first : first + count, :]
            s_hi, s_lo = slopes_ref[at, there, :], slopes_ref[at + 1, there, :]
            term = dot(hi, s_hi) + dot(hi, s_lo) + dot(lo, s_hi)
            total = term if total is None else total + term
        return total.T

    out_ref[:, :wide] = product(wide, wide, 0)
    out_ref[:, wide : wide + half] = product(0, half, 2) * scale
    out_ref[:, wide + half :] = product(half, half, 4) * scale


def add_moved(own_ref, moved_ref, *out_refs):
    rows = out_refs[0].shape[0]
    for n, out_ref in enumerate(out_refs):
        here = pl.ds(n * rows, rows)
        out_ref[...] = own_ref[here, :] + moved_ref[here, :]


def add_ring(*refs):
    *in_refs, near_ref, far_ref = refs
    total = in_refs[0][...]
    for ref in in_refs[1:]:
        total = total + ref[...]
    rows = near_ref.shape[0]
    near_ref[...] = total[:rows]
    far_ref[...] = total[rows:]


def add_pair(near_ref, came_ref, left_ref, right_ref):
    wide = left_ref.shape[1]
    total = near_ref[...] + came_ref[...]
    left_ref[...] = total[:, :wide]
    right_ref[...] = total[:, wide:]


def add_blocks(parts_ref, left_ref, right_ref):
    wide = left_ref.shape[1]
    total = jnp.sum(parts_ref[...], axis=0)
    left_ref[...] = total[:, :wide]
    right_ref[...] = total[:, wide:]


def swap(x, axis):
    return lax.ppermute(x, axis, [(0, 1), (1, 0)])


def around(x, step):
    return lax.ppermute(x, RING, [(n, (n + step) % AROUND) for n in range(AROUND)])


def exchange(x, axes):
    return lax.all_to_all(x, axes, 0, 0, tiled=True)


def per_device(queries, key_pair, values, grad_out):
    wide = values.shape[1]
    own_keys, own_rows = key_pair.shape[0], queries.shape[0]
    rows, columns = KEYS_IN * own_keys, QUERIES_IN * own_rows
    block = 4 * 2 * wide * rows
    kv = call(lay_once, shape(F32, own_keys, 2 * wide), 0, block // 4)(key_pair, values)
    qg = call(lay_out, shape(F32, QUERIES_IN, own_rows, 2 * wide), 0, block // 2)(queries, grad_out)
    kv_pair = call(stack, shape(F32, NEAR * own_keys, 2 * wide), 10**10, block // 2)(kv, swap(kv, PAIR))
    kv_own = [kv_pair] + [around(kv_pair, -n) for n in range(1, AROUND)]
    kv_other = [swap(x, CORE) for x in kv_own]
    qg_all = exchange(qg, QUERY_GROUP).reshape(columns, 2 * wide)
    split = call(
        split_keys,
        (shape(BF16, 3, rows, wide), shape(BF16, 2, rows, wide), shape(BF16, 2, 2 * wide, rows)),
        0,
        3 * block,
    )
    own_key, own_value, own_turned = split(*kv_own)
    other_key, other_value, other_turned = split(*kv_other)
    big = shape(F32, 2 * rows, columns)
    pairs = 2 * rows * columns
    w1, w2, dp, stats = call(
        forward, (big, big, big, shape(F32, QUERIES_IN, 8, columns)), 2 * pairs * wide * 9, 4 * pairs * 3
    )(own_key, own_value, other_key, other_value, qg_all)
    every = exchange(stats, QUERY_GROUP)
    half_grad = shape(F32, rows, 2 * wide)
    own, other, slopes = call(
        key_side,
        (half_grad, half_grad, shape(BF16, 6, 2 * rows, columns)),
        2 * pairs * wide * 6,
        4 * pairs * 6,
    )(w1, w2, dp, qg_all, stats, every)
    moved = swap(other, CORE)
    dq = call(query_side, shape(F32, columns, 2 * wide), 2 * pairs * wide * 6, 4 * pairs * 4)(
        slopes, own_turned, other_turned
    )
    dq_parts = exchange(dq.reshape(QUERIES_IN, own_rows, 2 * wide), QUERY_GROUP)
    attended, grad_queries = call(
        add_blocks, (shape(F32, own_rows, wide),) * 2, 0, block // 2
    )(dq_parts)
    mine, *away = call(add_moved, (shape(F32, NEAR * own_keys, 2 * wide),) * AROUND, 0, block)(own, moved)
    landed = [around(x, n + 1) for n, x in enumerate(away)]
    near, far = call(add_ring, (shape(F32, own_keys, 2 * wide),) * NEAR, 0, block)(mine, *landed)
    grad_keys, grad_values = call(add_pair, (shape(F32, own_keys, wide),) * 2, 0, block // 4)(near, swap(far, PAIR))
    return attended, grad_queries, grad_keys, grad_values


def solution(mesh):
    fine = Mesh(mesh.devices.reshape((2,) * 9), PB + KA)
    by_query, by_key = P(KA + PB, None), P(PB + KA, None)
    return jax.shard_map(
        per_device,
        mesh=fine,
        in_specs=(by_query, by_key, by_key, by_query),
        out_specs=(by_query, by_query, by_key, by_key),
        check_vma=False,
    )
```

```python
import functools

import jax
import jax.numpy as jnp
from jax import lax
from jax.experimental import pallas as pl
from jax.experimental.pallas import tpu as pltpu
from jax.sharding import Mesh, PartitionSpec as P

LAMBDA = 0.5
PB = ("z2", "z1", "z0", "xh")
KA = ("xl", "y2", "y1", "y0", "c")
RING = ("xh", "xl")
PAIR = "y0"
AROUND = 4
NEAR = 2
KEYS_IN = NEAR * AROUND
QUERY_GROUP = ("z2", "z1", "z0", "y2", "y1")
QUERIES_IN = 32
CORE = "c"
STRIP = 256
F32, BF16 = jnp.float32, jnp.bfloat16
VMEM_LIMIT = 16 * 1024 * 1024


def call(body, out_shape, flops, moved, **given):
    return pl.pallas_call(
        body,
        out_shape=out_shape,
        cost_estimate=pl.CostEstimate(flops=flops, bytes_accessed=moved, transcendentals=0),
        compiler_params=pltpu.CompilerParams(vmem_limit_bytes=VMEM_LIMIT),
        **given,
    )


def shape(dtype, *dims):
    return jax.ShapeDtypeStruct(dims, dtype)


def parts(x, count):
    out = []
    for _ in range(count):
        out.append(x.astype(BF16))
        x = x - out[-1].astype(F32)
    return out


def dot(left, right, dims=((1,), (0,))):
    return lax.dot_general(left, right, (dims, ((), ())), preferred_element_type=F32)


def beside(*blocks):
    return jnp.concatenate(blocks, axis=1)


def lay_out(queries_ref, grad_ref, key_ref, value_ref, kv_ref, qg_ref, row_ref, sems):
    wide = key_ref.shape[1]
    copies = [
        pltpu.make_async_copy(source, target.at[:, pl.ds(first, wide)], sems.at[n])
        for n, (source, target, first) in enumerate(
            (
                (queries_ref, row_ref, 0),
                (grad_ref, row_ref, wide),
                (key_ref, kv_ref, 0),
                (value_ref, kv_ref, wide),
            )
        )
    ]
    for copy in copies:
        copy.start()
    for copy in copies[:2]:
        copy.wait()
    rows = row_ref[...]
    for n in range(qg_ref.shape[0]):
        qg_ref[n] = rows
    for copy in copies[2:]:
        copy.wait()


def stack(*refs):
    *in_refs, out_ref = refs
    rows = in_refs[0].shape[0]
    for n, ref in enumerate(in_refs):
        out_ref[pl.ds(n * rows, rows), :] = ref[...]


def halves(row):
    middle = row.shape[1] // 2
    return [row[:, :middle], row[:, middle:]]


def turn(*refs):
    *in_refs, out_ref = refs
    rows = in_refs[0].shape[0]
    for at, ref in enumerate(in_refs):
        for n, part in enumerate(parts(ref[...].T, 2)):
            out_ref[n, :, pl.ds(at * rows, rows)] = part


def forward(*refs):
    *in_refs, qg_ref, w1_ref, w2_ref, dp_ref, stats_ref, top_ref = refs
    half = qg_ref.shape[1] // 4
    scale = half ** (-0.5)
    g_hi, g_lo = parts(qg_ref[:, 2 * half :], 2)
    query = []
    for first in (0, half):
        hi, mid, low = parts(qg_ref[:, first : first + half] * scale, 3)
        query.append((beside(hi, mid), beside(low, hi)))
    rows = 2 * in_refs[0].shape[0]
    across = ((1,), (1,))
    tops = [None, None]
    for at in range(len(in_refs) // 2):
        both = jnp.concatenate([in_refs[2 * at][...], in_refs[2 * at + 1][...]], axis=0)
        there = pl.ds(at * rows, rows)
        for head, w_ref in enumerate((w1_ref, w2_ref)):
            hi, mid, low = parts(both[:, head * half : (head + 1) * half], 3)
            main, rest = query[head]
            score = (
                dot(beside(hi, hi), main, across)
                + dot(beside(mid, mid), main, across)
                + dot(beside(hi, low), rest, across)
            )
            w_ref[there, :] = score
            top = jnp.max(score, axis=0, keepdims=True)
            tops[head] = top if tops[head] is None else jnp.maximum(tops[head], top)
        v_hi, v_lo = parts(both[:, 2 * half :], 2)
        dp_ref[there, :] = dot(v_hi, g_hi, across) + dot(v_hi, g_lo, across) + dot(v_lo, g_hi, across)
    numbers = []
    for head, w_ref in enumerate((w1_ref, w2_ref)):
        mass = jnp.zeros_like(tops[head])
        lean = jnp.zeros_like(tops[head])
        for start in range(0, w_ref.shape[0], STRIP):
            here = pl.ds(start, STRIP)
            weight = jnp.exp(w_ref[here, :] - tops[head])
            w_ref[here, :] = weight
            mass = mass + jnp.sum(weight, axis=0, keepdims=True)
            lean = lean + jnp.sum(weight * dp_ref[here, :], axis=0, keepdims=True)
        numbers += halves(tops[head] + jnp.log(mass)) + halves(lean / mass)
    stats = jnp.concatenate(numbers, axis=0)
    for n in range(stats_ref.shape[0]):
        stats_ref[n] = stats
    top_ref[...] = jnp.concatenate(tops, axis=0)


def key_side(first, w1_ref, w2_ref, dp_ref, qg_ref, top_ref, every_ref, out_ref, slopes_ref):
    half = qg_ref.shape[1] // 4
    scale = half ** (-0.5)
    rescale, delta = [], []
    for head in range(2):
        logs = beside(every_ref[:, 4 * head, :], every_ref[:, 4 * head + 1, :])
        means = beside(every_ref[:, 4 * head + 2, :], every_ref[:, 4 * head + 3, :])
        top = jnp.max(logs, axis=0, keepdims=True)
        share = jnp.exp(logs - top)
        total = jnp.sum(share, axis=0, keepdims=True)
        delta.append(jnp.sum(share * means, axis=0, keepdims=True) / total)
        rescale.append(jnp.exp(top_ref[head : head + 1, :] - top) / total)
    g_hi, g_lo = parts(qg_ref[:, 2 * half :], 2)
    query = [parts(qg_ref[:, at : at + half] * scale, 2) for at in (0, half)]
    for start in range(0, out_ref.shape[0], STRIP):
        here = pl.ds(start, STRIP)
        there = pl.ds(first + start, STRIP)
        dp = dp_ref[there, :]
        p1 = w1_ref[there, :] * rescale[0]
        p2 = w2_ref[there, :] * (-LAMBDA * rescale[1])
        slopes = (p1 * (dp - delta[0]), p2 * (dp - delta[1]))
        mix_hi, mix_lo = parts(p1 + p2, 2)
        slopes_ref[0, here, :] = mix_hi
        slopes_ref[1, here, :] = mix_lo
        for head in range(2):
            hi, lo = parts(slopes[head], 2)
            slopes_ref[2 + 2 * head, here, :] = hi
            slopes_ref[3 + 2 * head, here, :] = lo
            q_hi, q_lo = query[head]
            both = dot(hi, beside(q_hi, q_lo))
            out_ref[here, head * half : (head + 1) * half] = both[:, :half] + both[:, half:] + dot(lo, q_hi)
        out_ref[here, 2 * half :] = dot(mix_hi, g_hi) + dot(mix_hi, g_lo) + dot(mix_lo, g_hi)


def key_side_and_turn(first, count, *refs):
    blocks, rest = refs[:count], refs[count:]
    turn(*blocks, rest[-1])
    key_side(first, *rest[:-1])


def query_side(own_ref, other_ref, turned_ref, out_ref):
    rows = own_ref.shape[1]
    wide = turned_ref.shape[1] // 2
    half = wide // 2
    scale = half ** (-0.5)

    def product(first, count, at):
        total = None
        for which, slopes_ref in enumerate((own_ref, other_ref)):
            there = pl.ds(which * rows, rows)
            hi, lo = turned_ref[0, first : first + count, there], turned_ref[1, first : first + count, there]
            s_hi, s_lo = slopes_ref[at], slopes_ref[at + 1]
            term = dot(hi, s_hi) + dot(hi, s_lo) + dot(lo, s_hi)
            total = term if total is None else total + term
        return total.T

    out_ref[:, :wide] = product(wide, wide, 0)
    out_ref[:, wide : wide + half] = product(0, half, 2) * scale
    out_ref[:, wide + half :] = product(half, half, 4) * scale


def add_moved(own_ref, moved_ref, *out_refs):
    rows = out_refs[0].shape[0]
    for n, out_ref in enumerate(out_refs):
        here = pl.ds(n * rows, rows)
        out_ref[...] = own_ref[here, :] + moved_ref[here, :]


def add_two(left_ref, right_ref, out_ref):
    out_ref[...] = left_ref[...] + right_ref[...]


def add_ring(*refs):
    *in_refs, near_ref, far_ref = refs
    total = in_refs[0][...]
    for ref in in_refs[1:]:
        total = total + ref[...]
    rows = near_ref.shape[0]
    near_ref[...] = total[:rows]
    far_ref[...] = total[rows:]


def add_pair(near_ref, came_ref, left_ref, right_ref):
    wide = left_ref.shape[1]
    total = near_ref[...] + came_ref[...]
    left_ref[...] = total[:, :wide]
    right_ref[...] = total[:, wide:]


def add_blocks(parts_ref, left_ref, right_ref):
    wide = left_ref.shape[1]
    total = jnp.sum(parts_ref[...], axis=0)
    left_ref[...] = total[:, :wide]
    right_ref[...] = total[:, wide:]


def in_hbm(x):
    return pltpu.with_memory_space_constraint(x, pltpu.HBM)


def swap(x, axis):
    return lax.ppermute(x, axis, [(0, 1), (1, 0)])


def around(x, step):
    return lax.ppermute(x, RING, [(n, (n + step) % AROUND) for n in range(AROUND)])


def exchange(x, axes):
    return lax.all_to_all(x, axes, 0, 0, tiled=True)


def per_device(queries, key_pair, values, grad_out):
    wide = values.shape[1]
    own_keys, own_rows = key_pair.shape[0], queries.shape[0]
    rows, columns = KEYS_IN * own_keys, QUERIES_IN * own_rows
    block = 4 * 2 * wide * rows
    kv, qg = call(
        lay_out,
        (shape(F32, own_keys, 2 * wide), shape(F32, QUERIES_IN, own_rows, 2 * wide)),
        0,
        block // 2,
        in_specs=[pl.BlockSpec(memory_space=pltpu.HBM)] * 4,
        scratch_shapes=[pltpu.VMEM((own_rows, 2 * wide), F32), pltpu.SemaphoreType.DMA((4,))],
    )(*(in_hbm(x) for x in (queries, grad_out, key_pair, values)))
    kv_pair = call(stack, shape(F32, NEAR * own_keys, 2 * wide), 10**10, block // 2)(kv, swap(kv, PAIR))
    kv_own = [kv_pair] + [around(kv_pair, -n) for n in range(1, AROUND)]
    kv_other = [swap(x, CORE) for x in kv_own]
    qg_all = exchange(qg, QUERY_GROUP).reshape(columns, 2 * wide)
    big = shape(F32, 2 * rows, columns)
    pairs = 2 * rows * columns
    stats_shape = shape(F32, QUERIES_IN, 8, columns // 2)
    w1, w2, dp, stats, tops = call(
        forward, (big, big, big, stats_shape, shape(F32, 2, columns)), 2 * pairs * wide * 9, 4 * pairs * 3
    )(*kv_own, *kv_other, qg_all)
    every = exchange(stats, QUERY_GROUP)
    half_out = (shape(F32, rows, 2 * wide), shape(BF16, 6, rows, columns))
    other, other_slopes = call(
        functools.partial(key_side, rows), half_out, pairs * wide * 6, 4 * pairs * 3
    )(w1, w2, dp, qg_all, tops, every)
    moved = swap(other, CORE)
    own, own_slopes, turned = call(
        functools.partial(key_side_and_turn, 0, 2 * AROUND),
        half_out + (shape(BF16, 2, 2 * wide, 2 * rows),),
        pairs * wide * 6,
        4 * pairs * 3,
    )(*kv_own, *kv_other, w1, w2, dp, qg_all, tops, every)
    dq = call(query_side, shape(F32, columns, 2 * wide), 2 * pairs * wide * 6, 4 * pairs * 4)(
        own_slopes, other_slopes, turned
    )
    dq_parts = exchange(dq.reshape(QUERIES_IN, own_rows, 2 * wide), QUERY_GROUP)
    attended, grad_queries = call(
        add_blocks, (shape(F32, own_rows, wide),) * 2, 0, block // 2
    )(dq_parts)
    mine, *away = call(add_moved, (shape(F32, NEAR * own_keys, 2 * wide),) * AROUND, 0, block)(own, moved)
    right, across, left = (around(x, n + 1) for n, x in enumerate(away))
    mine = call(add_two, shape(F32, NEAR * own_keys, 2 * wide), 10**10, block)(mine, across)
    near, far = call(add_ring, (shape(F32, own_keys, 2 * wide),) * NEAR, 0, block)(mine, right, left)
    grad_keys, grad_values = call(add_pair, (shape(F32, own_keys, wide),) * 2, 0, block // 4)(near, swap(far, PAIR))
    return attended, grad_queries, grad_keys, grad_values


def solution(mesh):
    fine = Mesh(mesh.devices.reshape((2,) * 9), PB + KA)
    by_query, by_key = P(KA + PB, None), P(PB + KA, None)
    return jax.shard_map(
        per_device,
        mesh=fine,
        in_specs=(by_query, by_key, by_key, by_query),
        out_specs=(by_query, by_query, by_key, by_key),
        check_vma=False,
    )
```

```python
import functools

import jax
import jax.numpy as jnp
from jax import lax
from jax.experimental import pallas as pl
from jax.experimental.pallas import tpu as pltpu
from jax.sharding import Mesh, PartitionSpec as P

LAMBDA = 0.5
PB = ("z2", "z1", "z0", "xh")
KA = ("xl", "y2", "y1", "y0", "c")
RING = ("xh", "xl")
PAIR = "y0"
AROUND = 4
NEAR = 2
KEYS_IN = NEAR * AROUND
QUERY_GROUP = ("z2", "z1", "z0", "y2", "y1")
QUERIES_IN = 32
CORE = "c"
STRIP = 256
F32, BF16 = jnp.float32, jnp.bfloat16
VMEM_LIMIT = 16 * 1024 * 1024


def call(body, out_shape, flops, moved, **given):
    return pl.pallas_call(
        body,
        out_shape=out_shape,
        cost_estimate=pl.CostEstimate(flops=flops, bytes_accessed=moved, transcendentals=0),
        compiler_params=pltpu.CompilerParams(vmem_limit_bytes=VMEM_LIMIT),
        **given,
    )


def shape(dtype, *dims):
    return jax.ShapeDtypeStruct(dims, dtype)


def parts(x, count):
    out = []
    for _ in range(count):
        out.append(x.astype(BF16))
        x = x - out[-1].astype(F32)
    return out


def dot(left, right, dims=((1,), (0,))):
    return lax.dot_general(left, right, (dims, ((), ())), preferred_element_type=F32)


def beside(*blocks):
    return jnp.concatenate(blocks, axis=1)


def lay_out(queries_ref, grad_ref, key_ref, value_ref, kv_ref, qg_ref, row_ref, sems):
    wide = key_ref.shape[1]
    copies = [
        pltpu.make_async_copy(source, target.at[:, pl.ds(first, wide)], sems.at[n])
        for n, (source, target, first) in enumerate(
            (
                (queries_ref, row_ref, 0),
                (grad_ref, row_ref, wide),
                (key_ref, kv_ref, 0),
                (value_ref, kv_ref, wide),
            )
        )
    ]
    for copy in copies:
        copy.start()
    for copy in copies[:2]:
        copy.wait()
    rows = row_ref[...]
    for n in range(qg_ref.shape[0]):
        qg_ref[n] = rows
    for copy in copies[2:]:
        copy.wait()


def stack(*refs):
    *in_refs, out_ref = refs
    rows = in_refs[0].shape[0]
    for n, ref in enumerate(in_refs):
        out_ref[pl.ds(n * rows, rows), :] = ref[...]


def halves(row):
    middle = row.shape[1] // 2
    return [row[:, :middle], row[:, middle:]]


def turn(*refs):
    *in_refs, out_ref = refs
    at = 0
    for ref in in_refs:
        rows = ref.shape[0]
        for n, part in enumerate(parts(ref[...].T, 2)):
            out_ref[n, :, pl.ds(at, rows)] = part
        at += rows


def forward(*refs):
    *in_refs, qg_ref, w1_ref, w2_ref, dp_ref, stats_ref, top_ref = refs
    half = qg_ref.shape[1] // 4
    scale = half ** (-0.5)
    g_hi, g_lo = parts(qg_ref[:, 2 * half :], 2)
    query = []
    for first in (0, half):
        hi, mid, low = parts(qg_ref[:, first : first + half] * scale, 3)
        query.append((beside(hi, mid), beside(low, hi)))
    across = ((1,), (1,))
    tops = [None, None]
    at = 0
    for some in (in_refs[0:1], in_refs[1:3], in_refs[3:4], in_refs[4:6]):
        both = jnp.concatenate([ref[...] for ref in some], axis=0)
        there = pl.ds(at, both.shape[0])
        at += both.shape[0]
        for head, w_ref in enumerate((w1_ref, w2_ref)):
            hi, mid, low = parts(both[:, head * half : (head + 1) * half], 3)
            main, rest = query[head]
            score = (
                dot(beside(hi, hi), main, across)
                + dot(beside(mid, mid), main, across)
                + dot(beside(hi, low), rest, across)
            )
            w_ref[there, :] = score
            top = jnp.max(score, axis=0, keepdims=True)
            tops[head] = top if tops[head] is None else jnp.maximum(tops[head], top)
        v_hi, v_lo = parts(both[:, 2 * half :], 2)
        dp_ref[there, :] = dot(v_hi, g_hi, across) + dot(v_hi, g_lo, across) + dot(v_lo, g_hi, across)
    numbers = []
    for head, w_ref in enumerate((w1_ref, w2_ref)):
        mass = jnp.zeros_like(tops[head])
        lean = jnp.zeros_like(tops[head])
        for start in range(0, w_ref.shape[0], STRIP):
            here = pl.ds(start, STRIP)
            weight = jnp.exp(w_ref[here, :] - tops[head])
            w_ref[here, :] = weight
            mass = mass + jnp.sum(weight, axis=0, keepdims=True)
            lean = lean + jnp.sum(weight * dp_ref[here, :], axis=0, keepdims=True)
        numbers += halves(tops[head] + jnp.log(mass)) + halves(lean / mass)
    stats = jnp.concatenate(numbers, axis=0)
    for n in range(stats_ref.shape[0]):
        stats_ref[n] = stats
    top_ref[...] = jnp.concatenate(tops, axis=0)


def key_side(first, w1_ref, w2_ref, dp_ref, qg_ref, top_ref, every_ref, out_ref, slopes_ref):
    half = qg_ref.shape[1] // 4
    scale = half ** (-0.5)
    rescale, delta = [], []
    for head in range(2):
        logs = beside(every_ref[:, 4 * head, :], every_ref[:, 4 * head + 1, :])
        means = beside(every_ref[:, 4 * head + 2, :], every_ref[:, 4 * head + 3, :])
        top = jnp.max(logs, axis=0, keepdims=True)
        share = jnp.exp(logs - top)
        total = jnp.sum(share, axis=0, keepdims=True)
        delta.append(jnp.sum(share * means, axis=0, keepdims=True) / total)
        rescale.append(jnp.exp(top_ref[head : head + 1, :] - top) / total)
    g_hi, g_lo = parts(qg_ref[:, 2 * half :], 2)
    query = [parts(qg_ref[:, at : at + half] * scale, 2) for at in (0, half)]
    for start in range(0, out_ref.shape[0], STRIP):
        here = pl.ds(start, STRIP)
        there = pl.ds(first + start, STRIP)
        dp = dp_ref[there, :]
        p1 = w1_ref[there, :] * rescale[0]
        p2 = w2_ref[there, :] * (-LAMBDA * rescale[1])
        slopes = (p1 * (dp - delta[0]), p2 * (dp - delta[1]))
        mix_hi, mix_lo = parts(p1 + p2, 2)
        slopes_ref[0, here, :] = mix_hi
        slopes_ref[1, here, :] = mix_lo
        for head in range(2):
            hi, lo = parts(slopes[head], 2)
            slopes_ref[2 + 2 * head, here, :] = hi
            slopes_ref[3 + 2 * head, here, :] = lo
            q_hi, q_lo = query[head]
            both = dot(hi, beside(q_hi, q_lo))
            out_ref[here, head * half : (head + 1) * half] = both[:, :half] + both[:, half:] + dot(lo, q_hi)
        out_ref[here, 2 * half :] = dot(mix_hi, g_hi) + dot(mix_hi, g_lo) + dot(mix_lo, g_hi)


def query_side(own_ref, other_ref, turned_ref, out_ref):
    rows = own_ref.shape[1]
    wide = turned_ref.shape[1] // 2
    half = wide // 2
    scale = half ** (-0.5)

    def product(first, count, at):
        total = None
        for which, slopes_ref in enumerate((own_ref, other_ref)):
            there = pl.ds(which * rows, rows)
            hi, lo = turned_ref[0, first : first + count, there], turned_ref[1, first : first + count, there]
            s_hi, s_lo = slopes_ref[at], slopes_ref[at + 1]
            term = dot(hi, s_hi) + dot(hi, s_lo) + dot(lo, s_hi)
            total = term if total is None else total + term
        return total.T

    out_ref[:, :wide] = product(wide, wide, 0)
    out_ref[:, wide : wide + half] = product(0, half, 2) * scale
    out_ref[:, wide + half :] = product(half, half, 4) * scale


def add_moved(own_ref, moved_ref, _, *refs):
    *out_refs, _ = refs
    rows = out_refs[0].shape[0]
    for n, out_ref in enumerate(out_refs):
        here = pl.ds(n * rows, rows)
        out_ref[...] = own_ref[here, :] + moved_ref[here, :]


def own_half(count, *refs):
    blocks = refs[:count]
    *given, other_slopes, out_ref, dq_ref, slopes, turned = refs[count:]
    key_side(0, *given, out_ref, slopes)
    turn(*blocks, turned)
    query_side(slopes, other_slopes, turned, dq_ref)


def add_two(left_ref, right_ref, out_ref):
    out_ref[...] = left_ref[...] + right_ref[...]


def add_ring(*refs):
    *in_refs, near_ref, far_ref = refs
    total = in_refs[0][...]
    for ref in in_refs[1:]:
        total = total + ref[...]
    rows = near_ref.shape[0]
    near_ref[...] = total[:rows]
    far_ref[...] = total[rows:]


def finish(near_ref, came_ref, parts_ref, keys_ref, values_ref, attended_ref, queries_ref):
    wide = keys_ref.shape[1]
    total = near_ref[...] + came_ref[...]
    keys_ref[...] = total[:, :wide]
    values_ref[...] = total[:, wide:]
    total = jnp.sum(parts_ref[...], axis=0)
    attended_ref[...] = total[:, :wide]
    queries_ref[...] = total[:, wide:]


def in_hbm(x):
    return pltpu.with_memory_space_constraint(x, pltpu.HBM)


def swap(x, axis):
    return lax.ppermute(x, axis, [(0, 1), (1, 0)])


def around(x, step):
    return lax.ppermute(x, RING, [(n, (n + step) % AROUND) for n in range(AROUND)])


def exchange(x, axes):
    return lax.all_to_all(x, axes, 0, 0, tiled=True)


def per_device(queries, key_pair, values, grad_out):
    wide = values.shape[1]
    own_keys, own_rows = key_pair.shape[0], queries.shape[0]
    rows, columns = KEYS_IN * own_keys, QUERIES_IN * own_rows
    block = 4 * 2 * wide * rows
    kv, qg = call(
        lay_out,
        (shape(F32, own_keys, 2 * wide), shape(F32, QUERIES_IN, own_rows, 2 * wide)),
        0,
        block // 2,
        in_specs=[pl.BlockSpec(memory_space=pltpu.HBM)] * 4,
        scratch_shapes=[pltpu.VMEM((own_rows, 2 * wide), F32), pltpu.SemaphoreType.DMA((4,))],
    )(*(in_hbm(x) for x in (queries, grad_out, key_pair, values)))
    kv_pair = call(stack, shape(F32, NEAR * own_keys, 2 * wide), 10**10, block // 2)(kv, swap(kv, PAIR))
    right, across, left = (around(kv_pair, -n) for n in range(1, AROUND))
    first = call(stack, shape(F32, 2 * NEAR * own_keys, 2 * wide), 10**9, block)(kv_pair, across)
    kv_own = [first, right, left]
    kv_other = [swap(x, CORE) for x in kv_own]
    qg_all = exchange(qg, QUERY_GROUP).reshape(columns, 2 * wide)
    big = shape(F32, 2 * rows, columns)
    pairs = 2 * rows * columns
    stats_shape = shape(F32, QUERIES_IN, 8, columns // 2)
    w1, w2, dp, stats, tops = call(
        forward, (big, big, big, stats_shape, shape(F32, 2, columns)), 2 * pairs * wide * 9, 4 * pairs * 3
    )(*kv_own, *kv_other, qg_all)
    every = exchange(stats, QUERY_GROUP)
    half_out = (shape(F32, rows, 2 * wide), shape(BF16, 6, rows, columns))
    other, other_slopes = call(
        functools.partial(key_side, rows), half_out, pairs * wide * 6, 4 * pairs * 3
    )(w1, w2, dp, qg_all, tops, every)
    moved = swap(other, CORE)
    own, dq = call(
        functools.partial(own_half, 6),
        (shape(F32, rows, 2 * wide), shape(F32, columns, 2 * wide)),
        3 * pairs * wide * 6,
        4 * pairs * 4,
        scratch_shapes=[pltpu.VMEM((6, rows, columns), BF16), pltpu.VMEM((2, 2 * wide, 2 * rows), BF16)],
    )(*kv_own, *kv_other, w1, w2, dp, qg_all, tops, every, other_slopes)
    vmem, anywhere = pl.BlockSpec(memory_space=pltpu.VMEM), pl.BlockSpec(memory_space=pl.ANY)
    mine, *away, dq = call(
        add_moved,
        (shape(F32, NEAR * own_keys, 2 * wide),) * AROUND + (shape(F32, columns, 2 * wide),),
        0,
        block,
        in_specs=[vmem, vmem, anywhere],
        out_specs=[vmem] * AROUND + [anywhere],
        input_output_aliases={2: AROUND},
    )(own, moved, dq)
    dq_parts = exchange(dq.reshape(QUERIES_IN, own_rows, 2 * wide), QUERY_GROUP)
    across, right, left = (around(x, step) for x, step in zip(away, (2, 1, 3)))
    mine = call(add_two, shape(F32, NEAR * own_keys, 2 * wide), 10**9, block)(mine, across)
    near, far = call(add_ring, (shape(F32, own_keys, 2 * wide),) * NEAR, 0, block)(mine, right, left)
    grad_keys, grad_values, attended, grad_queries = call(
        finish, (shape(F32, own_keys, wide),) * 2 + (shape(F32, own_rows, wide),) * 2, 0, block
    )(near, swap(far, PAIR), dq_parts)
    return attended, grad_queries, grad_keys, grad_values


def solution(mesh):
    fine = Mesh(mesh.devices.reshape((2,) * 9), PB + KA)
    by_query, by_key = P(KA + PB, None), P(PB + KA, None)
    return jax.shard_map(
        per_device,
        mesh=fine,
        in_specs=(by_query, by_key, by_key, by_query),
        out_specs=(by_query, by_query, by_key, by_key),
        check_vma=False,
    )
```

```python
import functools

import jax
import jax.numpy as jnp
from jax import lax
from jax.experimental import pallas as pl
from jax.experimental.pallas import tpu as pltpu
from jax.sharding import Mesh, PartitionSpec as P

LAMBDA = 0.5
PB = ("z2", "z1", "z0", "xh")
KA = ("xl", "y2", "y1", "y0", "c")
RING = ("xh", "xl")
PAIR = "y0"
AROUND = 4
NEAR = 2
KEYS_IN = NEAR * AROUND
QUERY_GROUP = ("z2", "z1", "z0", "y2", "y1")
QUERIES_IN = 32
CORE = "c"
STRIP = 256
F32, BF16 = jnp.float32, jnp.bfloat16
VMEM_LIMIT = 16 * 1024 * 1024


def call(body, out_shape, flops, moved, **given):
    return pl.pallas_call(
        body,
        out_shape=out_shape,
        cost_estimate=pl.CostEstimate(flops=flops, bytes_accessed=moved, transcendentals=0),
        compiler_params=pltpu.CompilerParams(vmem_limit_bytes=VMEM_LIMIT),
        **given,
    )


def shape(dtype, *dims):
    return jax.ShapeDtypeStruct(dims, dtype)


def parts(x, count):
    out = []
    for _ in range(count):
        out.append(x.astype(BF16))
        x = x - out[-1].astype(F32)
    return out


def dot(left, right, dims=((1,), (0,))):
    return lax.dot_general(left, right, (dims, ((), ())), preferred_element_type=F32)


def beside(*blocks):
    return jnp.concatenate(blocks, axis=1)


def lay_out(queries_ref, grad_ref, key_ref, value_ref, kv_ref, qg_ref, row_ref, sems):
    wide = key_ref.shape[1]
    copies = [
        pltpu.make_async_copy(source, target.at[:, pl.ds(first, wide)], sems.at[n])
        for n, (source, target, first) in enumerate(
            (
                (queries_ref, row_ref, 0),
                (grad_ref, row_ref, wide),
                (key_ref, kv_ref, 0),
                (value_ref, kv_ref, wide),
            )
        )
    ]
    for copy in copies:
        copy.start()
    for copy in copies[:2]:
        copy.wait()
    rows = row_ref[...]
    for n in range(qg_ref.shape[0]):
        qg_ref[n] = rows
    for copy in copies[2:]:
        copy.wait()


def stack(*refs):
    *in_refs, out_ref = refs
    rows = in_refs[0].shape[0]
    for n, ref in enumerate(in_refs):
        out_ref[pl.ds(n * rows, rows), :] = ref[...]


def halves(row):
    middle = row.shape[1] // 2
    return [row[:, :middle], row[:, middle:]]


def turn(*refs):
    *in_refs, out_ref = refs
    at = 0
    for ref in in_refs:
        rows = ref.shape[0]
        for n, part in enumerate(parts(ref[...].T, 2)):
            out_ref[n, :, pl.ds(at, rows)] = part
        at += rows


def forward(*refs):
    *in_refs, qg_ref, w1_ref, w2_ref, dp_ref, stats_ref, top_ref = refs
    half = qg_ref.shape[1] // 4
    scale = half ** (-0.5)
    g_hi, g_lo = parts(qg_ref[:, 2 * half :], 2)
    query = []
    for first in (0, half):
        hi, mid, low = parts(qg_ref[:, first : first + half] * scale, 3)
        query.append((beside(hi, mid), beside(low, hi)))
    across = ((1,), (1,))
    tops = [None, None]
    for at, ref in enumerate(in_refs):
        both = ref[...]
        there = pl.ds(at * both.shape[0], both.shape[0])
        for head, w_ref in enumerate((w1_ref, w2_ref)):
            hi, mid, low = parts(both[:, head * half : (head + 1) * half], 3)
            main, rest = query[head]
            score = (
                dot(beside(hi, hi), main, across)
                + dot(beside(mid, mid), main, across)
                + dot(beside(hi, low), rest, across)
            )
            w_ref[there, :] = score
            top = jnp.max(score, axis=0, keepdims=True)
            tops[head] = top if tops[head] is None else jnp.maximum(tops[head], top)
        v_hi, v_lo = parts(both[:, 2 * half :], 2)
        dp_ref[there, :] = dot(v_hi, g_hi, across) + dot(v_hi, g_lo, across) + dot(v_lo, g_hi, across)
    numbers = []
    for head, w_ref in enumerate((w1_ref, w2_ref)):
        mass = jnp.zeros_like(tops[head])
        lean = jnp.zeros_like(tops[head])
        for start in range(0, w_ref.shape[0], STRIP):
            here = pl.ds(start, STRIP)
            weight = jnp.exp(w_ref[here, :] - tops[head])
            w_ref[here, :] = weight
            mass = mass + jnp.sum(weight, axis=0, keepdims=True)
            lean = lean + jnp.sum(weight * dp_ref[here, :], axis=0, keepdims=True)
        numbers += halves(tops[head] + jnp.log(mass)) + halves(lean / mass)
    stats = jnp.concatenate(numbers, axis=0)
    for n in range(stats_ref.shape[0]):
        stats_ref[n] = stats
    top_ref[...] = jnp.concatenate(tops, axis=0)


def key_side(first, w1_ref, w2_ref, dp_ref, qg_ref, top_ref, every_ref, out_ref, slopes_ref):
    half = qg_ref.shape[1] // 4
    scale = half ** (-0.5)
    rescale, delta = [], []
    for head in range(2):
        logs = beside(every_ref[:, 4 * head, :], every_ref[:, 4 * head + 1, :])
        means = beside(every_ref[:, 4 * head + 2, :], every_ref[:, 4 * head + 3, :])
        top = jnp.max(logs, axis=0, keepdims=True)
        share = jnp.exp(logs - top)
        total = jnp.sum(share, axis=0, keepdims=True)
        delta.append(jnp.sum(share * means, axis=0, keepdims=True) / total)
        rescale.append(jnp.exp(top_ref[head : head + 1, :] - top) / total)
    g_hi, g_lo = parts(qg_ref[:, 2 * half :], 2)
    query = [parts(qg_ref[:, at : at + half] * scale, 2) for at in (0, half)]
    for start in range(0, out_ref.shape[0], STRIP):
        here = pl.ds(start, STRIP)
        there = pl.ds(first + start, STRIP)
        dp = dp_ref[there, :]
        p1 = w1_ref[there, :] * rescale[0]
        p2 = w2_ref[there, :] * (-LAMBDA * rescale[1])
        slopes = (p1 * (dp - delta[0]), p2 * (dp - delta[1]))
        mix_hi, mix_lo = parts(p1 + p2, 2)
        slopes_ref[0, here, :] = mix_hi
        slopes_ref[1, here, :] = mix_lo
        for head in range(2):
            hi, lo = parts(slopes[head], 2)
            slopes_ref[2 + 2 * head, here, :] = hi
            slopes_ref[3 + 2 * head, here, :] = lo
            q_hi, q_lo = query[head]
            both = dot(hi, beside(q_hi, q_lo))
            out_ref[here, head * half : (head + 1) * half] = both[:, :half] + both[:, half:] + dot(lo, q_hi)
        out_ref[here, 2 * half :] = dot(mix_hi, g_hi) + dot(mix_hi, g_lo) + dot(mix_lo, g_hi)


def query_side(own_ref, other_ref, turned_ref, out_ref):
    rows = own_ref.shape[1]
    wide = turned_ref.shape[1] // 2
    half = wide // 2
    scale = half ** (-0.5)

    def product(first, count, at):
        total = None
        for which, slopes_ref in enumerate((own_ref, other_ref)):
            there = pl.ds(which * rows, rows)
            hi, lo = turned_ref[0, first : first + count, there], turned_ref[1, first : first + count, there]
            s_hi, s_lo = slopes_ref[at], slopes_ref[at + 1]
            term = dot(hi, s_hi) + dot(hi, s_lo) + dot(lo, s_hi)
            total = term if total is None else total + term
        return total.T

    out_ref[:, :wide] = product(wide, wide, 0)
    out_ref[:, wide : wide + half] = product(0, half, 2) * scale
    out_ref[:, wide + half :] = product(half, half, 4) * scale


def add_moved(own_ref, moved_ref, _, *refs):
    *out_refs, _ = refs
    rows = out_refs[0].shape[0]
    for n, out_ref in enumerate(out_refs):
        here = pl.ds(n * rows, rows)
        out_ref[...] = own_ref[here, :] + moved_ref[here, :]


def own_half(count, *refs):
    blocks = refs[:count]
    *given, other_slopes, out_ref, dq_ref, slopes, turned = refs[count:]
    key_side(0, *given, out_ref, slopes)
    turn(*blocks, turned)
    query_side(slopes, other_slopes, turned, dq_ref)


def add_two(left_ref, right_ref, out_ref):
    out_ref[...] = left_ref[...] + right_ref[...]


def add_ring(*refs):
    *in_refs, near_ref, far_ref = refs
    total = in_refs[0][...]
    for ref in in_refs[1:]:
        total = total + ref[...]
    rows = near_ref.shape[0]
    near_ref[...] = total[:rows]
    far_ref[...] = total[rows:]


def finish(near_ref, came_ref, parts_ref, keys_ref, values_ref, attended_ref, queries_ref):
    wide = keys_ref.shape[1]
    total = near_ref[...] + came_ref[...]
    keys_ref[...] = total[:, :wide]
    values_ref[...] = total[:, wide:]
    total = jnp.sum(parts_ref[...], axis=0)
    attended_ref[...] = total[:, :wide]
    queries_ref[...] = total[:, wide:]


def in_hbm(x):
    return pltpu.with_memory_space_constraint(x, pltpu.HBM)


def swap(x, axis):
    return lax.ppermute(x, axis, [(0, 1), (1, 0)])


def across(x):
    return lax.ppermute(x, RING, [(n, (n + AROUND // 2) % AROUND) for n in range(AROUND)])


def toward(x, step):
    pairs = [(2 * n + c, 2 * ((n + (step, -step)[c]) % AROUND) + c) for n in range(AROUND) for c in range(2)]
    return lax.ppermute(x, RING + (CORE,), pairs)


def exchange(x, axes):
    return lax.all_to_all(x, axes, 0, 0, tiled=True)


def per_device(queries, key_pair, values, grad_out):
    wide = values.shape[1]
    own_keys, own_rows = key_pair.shape[0], queries.shape[0]
    rows, columns = KEYS_IN * own_keys, QUERIES_IN * own_rows
    block = 4 * 2 * wide * rows
    kv, qg = call(
        lay_out,
        (shape(F32, own_keys, 2 * wide), shape(F32, QUERIES_IN, own_rows, 2 * wide)),
        0,
        block // 2,
        in_specs=[pl.BlockSpec(memory_space=pltpu.HBM)] * 4,
        scratch_shapes=[pltpu.VMEM((own_rows, 2 * wide), F32), pltpu.SemaphoreType.DMA((4,))],
    )(*(in_hbm(x) for x in (queries, grad_out, key_pair, values)))
    kv_pair = call(stack, shape(F32, NEAR * own_keys, 2 * wide), 10**10, block // 2)(kv, swap(kv, PAIR))
    far, right, left = across(kv_pair), toward(kv_pair, -1), toward(kv_pair, 1)
    first = call(stack, shape(F32, 2 * NEAR * own_keys, 2 * wide), 10**9, block)(kv_pair, far)
    second = call(stack, shape(F32, 2 * NEAR * own_keys, 2 * wide), 0, block)(right, left)
    kv_own = [first, second]
    kv_other = [swap(x, CORE) for x in kv_own]
    qg_all = exchange(qg, QUERY_GROUP).reshape(columns, 2 * wide)
    big = shape(F32, 2 * rows, columns)
    pairs = 2 * rows * columns
    stats_shape = shape(F32, QUERIES_IN, 8, columns // 2)
    w1, w2, dp, stats, tops = call(
        forward, (big, big, big, stats_shape, shape(F32, 2, columns)), 2 * pairs * wide * 9, 4 * pairs * 3
    )(*kv_own, *kv_other, qg_all)
    every = exchange(stats, QUERY_GROUP)
    half_out = (shape(F32, rows, 2 * wide), shape(BF16, 6, rows, columns))
    other, other_slopes = call(
        functools.partial(key_side, rows), half_out, pairs * wide * 6, 4 * pairs * 3
    )(w1, w2, dp, qg_all, tops, every)
    moved = swap(other, CORE)
    own, dq = call(
        functools.partial(own_half, 4),
        (shape(F32, rows, 2 * wide), shape(F32, columns, 2 * wide)),
        3 * pairs * wide * 6,
        4 * pairs * 4,
        scratch_shapes=[pltpu.VMEM((6, rows, columns), BF16), pltpu.VMEM((2, 2 * wide, 2 * rows), BF16)],
    )(*kv_own, *kv_other, w1, w2, dp, qg_all, tops, every, other_slopes)
    vmem, anywhere = pl.BlockSpec(memory_space=pltpu.VMEM), pl.BlockSpec(memory_space=pl.ANY)
    mine, *away, dq = call(
        add_moved,
        (shape(F32, NEAR * own_keys, 2 * wide),) * AROUND + (shape(F32, columns, 2 * wide),),
        0,
        block,
        in_specs=[vmem, vmem, anywhere],
        out_specs=[vmem] * AROUND + [anywhere],
        input_output_aliases={2: AROUND},
    )(own, moved, dq)
    dq_parts = exchange(dq.reshape(QUERIES_IN, own_rows, 2 * wide), QUERY_GROUP)
    far, right, left = across(away[0]), toward(away[1], 1), toward(away[2], -1)
    mine = call(add_two, shape(F32, NEAR * own_keys, 2 * wide), 10**9, block)(mine, far)
    near, beyond = call(add_ring, (shape(F32, own_keys, 2 * wide),) * NEAR, 0, block)(mine, right, left)
    grad_keys, grad_values, attended, grad_queries = call(
        finish, (shape(F32, own_keys, wide),) * 2 + (shape(F32, own_rows, wide),) * 2, 0, block
    )(near, swap(beyond, PAIR), dq_parts)
    return attended, grad_queries, grad_keys, grad_values


def solution(mesh):
    fine = Mesh(mesh.devices.reshape((2,) * 9), PB + KA)
    by_query, by_key = P(KA + PB, None), P(PB + KA, None)
    return jax.shard_map(
        per_device,
        mesh=fine,
        in_specs=(by_query, by_key, by_key, by_query),
        out_specs=(by_query, by_query, by_key, by_key),
        check_vma=False,
    )
```

```python
import functools

import jax
import jax.numpy as jnp
from jax import lax
from jax.experimental import pallas as pl
from jax.experimental.pallas import tpu as pltpu
from jax.sharding import Mesh, PartitionSpec as P

LAMBDA = 0.5
PB = ("z2", "z1", "z0", "xh")
KA = ("xl", "y2", "y1", "y0", "c")
RING = ("xh", "xl")
PAIR = "y0"
AROUND = 4
NEAR = 2
KEYS_IN = NEAR * AROUND
QUERY_GROUP = ("z2", "z1", "z0", "y2", "y1")
QUERIES_IN = 32
CORE = "c"
STRIP = 256
F32, BF16 = jnp.float32, jnp.bfloat16
VMEM_LIMIT = 16 * 1024 * 1024


def call(body, out_shape, flops, moved, **given):
    return pl.pallas_call(
        body,
        out_shape=out_shape,
        cost_estimate=pl.CostEstimate(flops=flops, bytes_accessed=moved, transcendentals=0),
        compiler_params=pltpu.CompilerParams(vmem_limit_bytes=VMEM_LIMIT),
        **given,
    )


def shape(dtype, *dims):
    return jax.ShapeDtypeStruct(dims, dtype)


def parts(x, count):
    out = []
    for _ in range(count):
        out.append(x.astype(BF16))
        x = x - out[-1].astype(F32)
    return out


def dot(left, right, dims=((1,), (0,))):
    return lax.dot_general(left, right, (dims, ((), ())), preferred_element_type=F32)


def beside(*blocks):
    return jnp.concatenate(blocks, axis=1)


def lay_out(queries_ref, grad_ref, key_ref, value_ref, kv_ref, qg_ref, row_ref, sems):
    wide = key_ref.shape[1]
    copies = [
        pltpu.make_async_copy(source, target.at[:, pl.ds(first, wide)], sems.at[n])
        for n, (source, target, first) in enumerate(
            (
                (queries_ref, row_ref, 0),
                (grad_ref, row_ref, wide),
                (key_ref, kv_ref, 0),
                (value_ref, kv_ref, wide),
            )
        )
    ]
    for copy in copies:
        copy.start()
    for copy in copies[:2]:
        copy.wait()
    rows = row_ref[...]
    for n in range(qg_ref.shape[0]):
        qg_ref[n] = rows
    for copy in copies[2:]:
        copy.wait()


def stack(*refs):
    *in_refs, out_ref = refs
    rows = in_refs[0].shape[0]
    for n, ref in enumerate(in_refs):
        out_ref[pl.ds(n * rows, rows), :] = ref[...]


def halves(row):
    middle = row.shape[1] // 2
    return [row[:, :middle], row[:, middle:]]


def turn(*refs):
    *in_refs, out_ref = refs
    at = 0
    for ref in in_refs:
        rows = ref.shape[0]
        for n, part in enumerate(parts(ref[...].T, 2)):
            out_ref[n, :, pl.ds(at, rows)] = part
        at += rows


def forward(*refs):
    *in_refs, qg_ref, w1_ref, w2_ref, dp_ref, stats_ref, top_ref = refs
    half = qg_ref.shape[1] // 4
    scale = half ** (-0.5)
    g_hi, g_lo = parts(qg_ref[:, 2 * half :], 2)
    query = []
    for first in (0, half):
        hi, mid, low = parts(qg_ref[:, first : first + half] * scale, 3)
        query.append((beside(hi, mid), beside(low, hi)))
    across = ((1,), (1,))
    tops = [None, None]
    for at, ref in enumerate(in_refs):
        both = ref[...]
        there = pl.ds(at * both.shape[0], both.shape[0])
        for head, w_ref in enumerate((w1_ref, w2_ref)):
            hi, mid, low = parts(both[:, head * half : (head + 1) * half], 3)
            main, rest = query[head]
            score = (
                dot(beside(hi, hi), main, across)
                + dot(beside(mid, mid), main, across)
                + dot(beside(hi, low), rest, across)
            )
            w_ref[there, :] = score
            top = jnp.max(score, axis=0, keepdims=True)
            tops[head] = top if tops[head] is None else jnp.maximum(tops[head], top)
        v_hi, v_lo = parts(both[:, 2 * half :], 2)
        dp_ref[there, :] = dot(v_hi, g_hi, across) + dot(v_hi, g_lo, across) + dot(v_lo, g_hi, across)
    numbers = []
    for head, w_ref in enumerate((w1_ref, w2_ref)):
        mass = jnp.zeros_like(tops[head])
        lean = jnp.zeros_like(tops[head])
        for start in range(0, w_ref.shape[0], STRIP):
            here = pl.ds(start, STRIP)
            weight = jnp.exp(w_ref[here, :] - tops[head])
            w_ref[here, :] = weight
            mass = mass + jnp.sum(weight, axis=0, keepdims=True)
            lean = lean + jnp.sum(weight * dp_ref[here, :], axis=0, keepdims=True)
        numbers += halves(tops[head] + jnp.log(mass)) + halves(lean / mass)
    stats = jnp.concatenate(numbers, axis=0)
    for n in range(stats_ref.shape[0]):
        stats_ref[n] = stats
    top_ref[...] = jnp.concatenate(tops, axis=0)


def key_side(first, w1_ref, w2_ref, dp_ref, qg_ref, top_ref, every_ref, out_ref, slopes_ref):
    half = qg_ref.shape[1] // 4
    scale = half ** (-0.5)
    rescale, delta = [], []
    for head in range(2):
        logs = beside(every_ref[:, 4 * head, :], every_ref[:, 4 * head + 1, :])
        means = beside(every_ref[:, 4 * head + 2, :], every_ref[:, 4 * head + 3, :])
        top = jnp.max(logs, axis=0, keepdims=True)
        share = jnp.exp(logs - top)
        total = jnp.sum(share, axis=0, keepdims=True)
        delta.append(jnp.sum(share * means, axis=0, keepdims=True) / total)
        rescale.append(jnp.exp(top_ref[head : head + 1, :] - top) / total)
    g_hi, g_lo = parts(qg_ref[:, 2 * half :], 2)
    query = [parts(qg_ref[:, at : at + half] * scale, 2) for at in (0, half)]
    for start in range(0, out_ref.shape[0], STRIP):
        here = pl.ds(start, STRIP)
        there = pl.ds(first + start, STRIP)
        dp = dp_ref[there, :]
        p1 = w1_ref[there, :] * rescale[0]
        p2 = w2_ref[there, :] * (-LAMBDA * rescale[1])
        slopes = (p1 * (dp - delta[0]), p2 * (dp - delta[1]))
        mix_hi, mix_lo = parts(p1 + p2, 2)
        slopes_ref[0, here, :] = mix_hi
        slopes_ref[1, here, :] = mix_lo
        for head in range(2):
            hi, lo = parts(slopes[head], 2)
            slopes_ref[2 + 2 * head, here, :] = hi
            slopes_ref[3 + 2 * head, here, :] = lo
            q_hi, q_lo = query[head]
            both = dot(hi, beside(q_hi, q_lo))
            out_ref[here, head * half : (head + 1) * half] = both[:, :half] + both[:, half:] + dot(lo, q_hi)
        out_ref[here, 2 * half :] = dot(mix_hi, g_hi) + dot(mix_hi, g_lo) + dot(mix_lo, g_hi)


def query_side(own_ref, other_ref, turned_ref, out_ref):
    rows = own_ref.shape[1]
    wide = turned_ref.shape[1] // 2
    half = wide // 2
    scale = half ** (-0.5)

    def product(first, count, at):
        total = None
        for which, slopes_ref in enumerate((own_ref, other_ref)):
            there = pl.ds(which * rows, rows)
            hi, lo = turned_ref[0, first : first + count, there], turned_ref[1, first : first + count, there]
            s_hi, s_lo = slopes_ref[at], slopes_ref[at + 1]
            term = dot(hi, s_hi) + dot(hi, s_lo) + dot(lo, s_hi)
            total = term if total is None else total + term
        return total.T

    out_ref[:, :wide] = product(wide, wide, 0)
    out_ref[:, wide : wide + half] = product(0, half, 2) * scale
    out_ref[:, wide + half :] = product(half, half, 4) * scale


def add_moved(own_ref, moved_ref, _, *refs):
    *out_refs, _ = refs
    first = 0
    for out_ref in out_refs:
        here = pl.ds(first, out_ref.shape[0])
        first += out_ref.shape[0]
        out_ref[...] = own_ref[here, :] + moved_ref[here, :]


def own_half(count, *refs):
    blocks = refs[:count]
    *given, other_slopes, out_ref, dq_ref, slopes, turned = refs[count:]
    key_side(0, *given, out_ref, slopes)
    turn(*blocks, turned)
    query_side(slopes, other_slopes, turned, dq_ref)


def add_two(left_ref, right_ref, out_ref):
    out_ref[...] = left_ref[...] + right_ref[...]


def add_ring(*refs):
    *in_refs, near_ref, far_ref = refs
    total = in_refs[0][...]
    for ref in in_refs[1:]:
        total = total + ref[...]
    rows = near_ref.shape[0]
    near_ref[...] = total[:rows]
    far_ref[...] = total[rows:]


def finish(*refs):
    *in_refs, parts_ref, keys_ref, values_ref, attended_ref, queries_ref = refs
    wide = keys_ref.shape[1]
    total = in_refs[0][...]
    for ref in in_refs[1:]:
        total = total + ref[...]
    keys_ref[...] = total[:, :wide]
    values_ref[...] = total[:, wide:]
    total = jnp.sum(parts_ref[...], axis=0)
    attended_ref[...] = total[:, :wide]
    queries_ref[...] = total[:, wide:]


def in_hbm(x):
    return pltpu.with_memory_space_constraint(x, pltpu.HBM)


def swap(x, axis):
    return lax.ppermute(x, axis, [(0, 1), (1, 0)])


def across(x):
    return lax.ppermute(x, RING, [(n, (n + AROUND // 2) % AROUND) for n in range(AROUND)])


def toward(x, step):
    pairs = [(2 * n + c, 2 * ((n + (step, -step)[c]) % AROUND) + c) for n in range(AROUND) for c in range(2)]
    return lax.ppermute(x, RING + (CORE,), pairs)


def past(x, step):
    places = [(n, y, c) for n in range(AROUND) for y in range(NEAR) for c in range(2)]
    at = {place: n for n, place in enumerate(places)}
    pairs = [(at[n, y, c], at[(n + (step, -step)[c]) % AROUND, y ^ 1, c]) for n, y, c in places]
    return lax.ppermute(x, RING + (PAIR, CORE), pairs)


def exchange(x, axes):
    return lax.all_to_all(x, axes, 0, 0, tiled=True)


def per_device(queries, key_pair, values, grad_out):
    wide = values.shape[1]
    own_keys, own_rows = key_pair.shape[0], queries.shape[0]
    rows, columns = KEYS_IN * own_keys, QUERIES_IN * own_rows
    block = 4 * 2 * wide * rows
    kv, qg = call(
        lay_out,
        (shape(F32, own_keys, 2 * wide), shape(F32, QUERIES_IN, own_rows, 2 * wide)),
        0,
        block // 2,
        in_specs=[pl.BlockSpec(memory_space=pltpu.HBM)] * 4,
        scratch_shapes=[pltpu.VMEM((own_rows, 2 * wide), F32), pltpu.SemaphoreType.DMA((4,))],
    )(*(in_hbm(x) for x in (queries, grad_out, key_pair, values)))
    kv_pair = call(stack, shape(F32, NEAR * own_keys, 2 * wide), 10**10, block // 2)(kv, swap(kv, PAIR))
    far, right, left = across(kv_pair), toward(kv_pair, -1), toward(kv_pair, 1)
    first = call(stack, shape(F32, 2 * NEAR * own_keys, 2 * wide), 10**9, block)(kv_pair, far)
    second = call(stack, shape(F32, 2 * NEAR * own_keys, 2 * wide), 0, block)(right, left)
    kv_own = [first, second]
    kv_other = [swap(x, CORE) for x in kv_own]
    qg_all = exchange(qg, QUERY_GROUP).reshape(columns, 2 * wide)
    big = shape(F32, 2 * rows, columns)
    pairs = 2 * rows * columns
    stats_shape = shape(F32, QUERIES_IN, 8, columns // 2)
    w1, w2, dp, stats, tops = call(
        forward, (big, big, big, stats_shape, shape(F32, 2, columns)), 2 * pairs * wide * 9, 4 * pairs * 3
    )(*kv_own, *kv_other, qg_all)
    every = exchange(stats, QUERY_GROUP)
    half_out = (shape(F32, rows, 2 * wide), shape(BF16, 6, rows, columns))
    other, other_slopes = call(
        functools.partial(key_side, rows), half_out, pairs * wide * 6, 4 * pairs * 3
    )(w1, w2, dp, qg_all, tops, every)
    moved = swap(other, CORE)
    own, dq = call(
        functools.partial(own_half, 4),
        (shape(F32, rows, 2 * wide), shape(F32, columns, 2 * wide)),
        3 * pairs * wide * 6,
        4 * pairs * 4,
        scratch_shapes=[pltpu.VMEM((6, rows, columns), BF16), pltpu.VMEM((2, 2 * wide, 2 * rows), BF16)],
    )(*kv_own, *kv_other, w1, w2, dp, qg_all, tops, every, other_slopes)
    vmem, anywhere = pl.BlockSpec(memory_space=pltpu.VMEM), pl.BlockSpec(memory_space=pl.ANY)
    pair_sum, block_sum = shape(F32, NEAR * own_keys, 2 * wide), shape(F32, own_keys, 2 * wide)
    mine, far, right, left, left_past, dq = call(
        add_moved,
        (pair_sum,) * 3 + (block_sum,) * 2 + (shape(F32, columns, 2 * wide),),
        0,
        block,
        in_specs=[vmem, vmem, anywhere],
        out_specs=[vmem] * 5 + [anywhere],
        input_output_aliases={2: 5},
    )(own, moved, dq)
    dq_parts = exchange(dq.reshape(QUERIES_IN, own_rows, 2 * wide), QUERY_GROUP)
    sides = (toward(left, -1), past(left_past, -1))
    mine = call(add_two, pair_sum, 10**9, block)(mine, across(far))
    near, beyond = call(add_ring, (block_sum,) * NEAR, 0, block)(mine, toward(right, 1))
    grad_keys, grad_values, attended, grad_queries = call(
        finish, (shape(F32, own_keys, wide),) * 2 + (shape(F32, own_rows, wide),) * 2, 0, block
    )(near, *sides, swap(beyond, PAIR), dq_parts)
    return attended, grad_queries, grad_keys, grad_values


def solution(mesh):
    fine = Mesh(mesh.devices.reshape((2,) * 9), PB + KA)
    by_query, by_key = P(KA + PB, None), P(PB + KA, None)
    return jax.shard_map(
        per_device,
        mesh=fine,
        in_specs=(by_query, by_key, by_key, by_query),
        out_specs=(by_query, by_query, by_key, by_key),
        check_vma=False,
    )
```

```python
import functools

import jax
import jax.numpy as jnp
from jax import lax
from jax.experimental import pallas as pl
from jax.experimental.pallas import tpu as pltpu
from jax.sharding import Mesh, PartitionSpec as P

LAMBDA = 0.5
PB = ("z2", "z1", "z0", "xh")
KA = ("xl", "y2", "y1", "y0", "c")
RING = ("xh", "xl")
PAIR = "y0"
AROUND = 4
NEAR = 2
KEYS_IN = NEAR * AROUND
QUERY_GROUP = ("z2", "z1", "z0", "y2", "y1")
QUERIES_IN = 32
CORE = "c"
STRIP = 256
F32, BF16 = jnp.float32, jnp.bfloat16
VMEM_LIMIT = 16 * 1024 * 1024


def call(body, out_shape, flops, moved, **given):
    return pl.pallas_call(
        body,
        out_shape=out_shape,
        cost_estimate=pl.CostEstimate(flops=flops, bytes_accessed=moved, transcendentals=0),
        compiler_params=pltpu.CompilerParams(vmem_limit_bytes=VMEM_LIMIT),
        **given,
    )


def shape(dtype, *dims):
    return jax.ShapeDtypeStruct(dims, dtype)


def parts(x, count):
    out = []
    for _ in range(count):
        out.append(x.astype(BF16))
        x = x - out[-1].astype(F32)
    return out


def dot(left, right, dims=((1,), (0,))):
    return lax.dot_general(left, right, (dims, ((), ())), preferred_element_type=F32)


def beside(*blocks):
    return jnp.concatenate(blocks, axis=1)


def lay_out(queries_ref, grad_ref, key_ref, value_ref, kv_ref, qg_ref, row_ref, sems):
    wide = key_ref.shape[1]
    copies = [
        pltpu.make_async_copy(source, target.at[:, pl.ds(first, wide)], sems.at[n])
        for n, (source, target, first) in enumerate(
            (
                (queries_ref, row_ref, 0),
                (grad_ref, row_ref, wide),
                (key_ref, kv_ref, 0),
                (value_ref, kv_ref, wide),
            )
        )
    ]
    for copy in copies:
        copy.start()
    for copy in copies[:2]:
        copy.wait()
    rows = row_ref[...]
    for n in range(qg_ref.shape[0]):
        qg_ref[n] = rows
    for copy in copies[2:]:
        copy.wait()


def stack(*refs):
    *in_refs, out_ref = refs
    rows = in_refs[0].shape[0]
    for n, ref in enumerate(in_refs):
        out_ref[pl.ds(n * rows, rows), :] = ref[...]


def halves(row):
    middle = row.shape[1] // 2
    return [row[:, :middle], row[:, middle:]]


def turn(*refs):
    *in_refs, out_ref = refs
    at = 0
    for ref in in_refs:
        rows = ref.shape[0]
        for n, part in enumerate(parts(ref[...].T, 2)):
            out_ref[n, :, pl.ds(at, rows)] = part
        at += rows


def forward(*refs):
    *in_refs, qg_ref, w1_ref, w2_ref, dp_ref, stats_ref, top_ref = refs
    half = qg_ref.shape[1] // 4
    scale = half ** (-0.5)
    g_hi, g_lo = parts(qg_ref[:, 2 * half :], 2)
    query = []
    for first in (0, half):
        hi, mid, low = parts(qg_ref[:, first : first + half] * scale, 3)
        query.append((beside(hi, mid), beside(low, hi)))
    across = ((1,), (1,))
    tops = [None, None]
    for at, ref in enumerate(in_refs):
        both = ref[...]
        there = pl.ds(at * both.shape[0], both.shape[0])
        for head, w_ref in enumerate((w1_ref, w2_ref)):
            hi, mid, low = parts(both[:, head * half : (head + 1) * half], 3)
            main, rest = query[head]
            score = (
                dot(beside(hi, hi), main, across)
                + dot(beside(mid, mid), main, across)
                + dot(beside(hi, low), rest, across)
            )
            w_ref[there, :] = score
            top = jnp.max(score, axis=0, keepdims=True)
            tops[head] = top if tops[head] is None else jnp.maximum(tops[head], top)
        v_hi, v_lo = parts(both[:, 2 * half :], 2)
        dp_ref[there, :] = dot(v_hi, g_hi, across) + dot(v_hi, g_lo, across) + dot(v_lo, g_hi, across)
    numbers = []
    for head, w_ref in enumerate((w1_ref, w2_ref)):
        mass = jnp.zeros_like(tops[head])
        lean = jnp.zeros_like(tops[head])
        for start in range(0, w_ref.shape[0], STRIP):
            here = pl.ds(start, STRIP)
            weight = jnp.exp(w_ref[here, :] - tops[head])
            w_ref[here, :] = weight
            mass = mass + jnp.sum(weight, axis=0, keepdims=True)
            lean = lean + jnp.sum(weight * dp_ref[here, :], axis=0, keepdims=True)
        numbers += halves(tops[head] + jnp.log(mass)) + halves(lean / mass)
    stats = jnp.concatenate(numbers, axis=0)
    for n in range(stats_ref.shape[0]):
        stats_ref[n] = stats
    top_ref[...] = jnp.concatenate(tops, axis=0)


def key_side(first, w1_ref, w2_ref, dp_ref, qg_ref, top_ref, every_ref, out_ref, slopes_ref):
    half = qg_ref.shape[1] // 4
    scale = half ** (-0.5)
    rescale, delta = [], []
    for head in range(2):
        logs = beside(every_ref[:, 4 * head, :], every_ref[:, 4 * head + 1, :])
        means = beside(every_ref[:, 4 * head + 2, :], every_ref[:, 4 * head + 3, :])
        top = jnp.max(logs, axis=0, keepdims=True)
        share = jnp.exp(logs - top)
        total = jnp.sum(share, axis=0, keepdims=True)
        delta.append(jnp.sum(share * means, axis=0, keepdims=True) / total)
        rescale.append(jnp.exp(top_ref[head : head + 1, :] - top) / total)
    g_hi, g_lo = parts(qg_ref[:, 2 * half :], 2)
    query = [parts(qg_ref[:, at : at + half] * scale, 2) for at in (0, half)]
    for start in range(0, out_ref.shape[0], STRIP):
        here = pl.ds(start, STRIP)
        there = pl.ds(first + start, STRIP)
        dp = dp_ref[there, :]
        p1 = w1_ref[there, :] * rescale[0]
        p2 = w2_ref[there, :] * (-LAMBDA * rescale[1])
        slopes = (p1 * (dp - delta[0]), p2 * (dp - delta[1]))
        mix_hi, mix_lo = parts(p1 + p2, 2)
        slopes_ref[0, here, :] = mix_hi
        slopes_ref[1, here, :] = mix_lo
        for head in range(2):
            hi, lo = parts(slopes[head], 2)
            slopes_ref[2 + 2 * head, here, :] = hi
            slopes_ref[3 + 2 * head, here, :] = lo
            q_hi, q_lo = query[head]
            both = dot(hi, beside(q_hi, q_lo))
            out_ref[here, head * half : (head + 1) * half] = both[:, :half] + both[:, half:] + dot(lo, q_hi)
        out_ref[here, 2 * half :] = dot(mix_hi, g_hi) + dot(mix_hi, g_lo) + dot(mix_lo, g_hi)


def query_side(own_ref, other_ref, turned_ref, out_ref):
    rows = own_ref.shape[1]
    wide = turned_ref.shape[1] // 2
    half = wide // 2
    scale = half ** (-0.5)

    def product(first, count, at):
        total = None
        for which, slopes_ref in enumerate((own_ref, other_ref)):
            there = pl.ds(which * rows, rows)
            hi, lo = turned_ref[0, first : first + count, there], turned_ref[1, first : first + count, there]
            s_hi, s_lo = slopes_ref[at], slopes_ref[at + 1]
            term = dot(hi, s_hi) + dot(hi, s_lo) + dot(lo, s_hi)
            total = term if total is None else total + term
        return total.T

    out_ref[:, :wide] = product(wide, wide, 0)
    out_ref[:, wide : wide + half] = product(0, half, 2) * scale
    out_ref[:, wide + half :] = product(half, half, 4) * scale


def add_moved(own_ref, moved_ref, _, *refs):
    *out_refs, _ = refs
    first = 0
    for out_ref in out_refs:
        here = pl.ds(first, out_ref.shape[0])
        first += out_ref.shape[0]
        out_ref[...] = own_ref[here, :] + moved_ref[here, :]


def own_half(count, *refs):
    blocks = refs[:count]
    *given, other_slopes, out_ref, dq_ref, slopes, turned = refs[count:]
    key_side(0, *given, out_ref, slopes)
    turn(*blocks, turned)
    query_side(slopes, other_slopes, turned, dq_ref)


def add_ring(*refs):
    *in_refs, near_ref, far_ref = refs
    total = in_refs[0][...]
    for ref in in_refs[1:]:
        total = total + ref[...]
    rows = near_ref.shape[0]
    near_ref[...] = total[:rows]
    far_ref[...] = total[rows:]


def finish(*refs):
    *in_refs, parts_ref, keys_ref, values_ref, attended_ref, queries_ref = refs
    wide = keys_ref.shape[1]
    total = in_refs[0][...]
    for ref in in_refs[1:]:
        total = total + ref[...]
    keys_ref[...] = total[:, :wide]
    values_ref[...] = total[:, wide:]
    total = jnp.sum(parts_ref[...], axis=0)
    attended_ref[...] = total[:, :wide]
    queries_ref[...] = total[:, wide:]


def in_hbm(x):
    return pltpu.with_memory_space_constraint(x, pltpu.HBM)


def swap(x, axis):
    return lax.ppermute(x, axis, [(0, 1), (1, 0)])


def across(x):
    return lax.ppermute(x, RING, [(n, (n + AROUND // 2) % AROUND) for n in range(AROUND)])


def toward(x, step):
    pairs = [(2 * n + c, 2 * ((n + (step, -step)[c]) % AROUND) + c) for n in range(AROUND) for c in range(2)]
    return lax.ppermute(x, RING + (CORE,), pairs)


def past(x, step):
    places = [(n, y, c) for n in range(AROUND) for y in range(NEAR) for c in range(2)]
    at = {place: n for n, place in enumerate(places)}
    pairs = [(at[n, y, c], at[(n + (step, -step)[c]) % AROUND, y ^ 1, c]) for n, y, c in places]
    return lax.ppermute(x, RING + (PAIR, CORE), pairs)


def exchange(x, axes):
    return lax.all_to_all(x, axes, 0, 0, tiled=True)


def per_device(queries, key_pair, values, grad_out):
    wide = values.shape[1]
    own_keys, own_rows = key_pair.shape[0], queries.shape[0]
    rows, columns = KEYS_IN * own_keys, QUERIES_IN * own_rows
    block = 4 * 2 * wide * rows
    kv, qg = call(
        lay_out,
        (shape(F32, own_keys, 2 * wide), shape(F32, QUERIES_IN, own_rows, 2 * wide)),
        0,
        block // 2,
        in_specs=[pl.BlockSpec(memory_space=pltpu.HBM)] * 4,
        scratch_shapes=[pltpu.VMEM((own_rows, 2 * wide), F32), pltpu.SemaphoreType.DMA((4,))],
    )(*(in_hbm(x) for x in (queries, grad_out, key_pair, values)))
    kv_pair = call(stack, shape(F32, NEAR * own_keys, 2 * wide), 10**10, block // 2)(kv, swap(kv, PAIR))
    far, right, left = across(kv_pair), toward(kv_pair, -1), toward(kv_pair, 1)
    first = call(stack, shape(F32, 2 * NEAR * own_keys, 2 * wide), 10**9, block)(kv_pair, far)
    second = call(stack, shape(F32, 2 * NEAR * own_keys, 2 * wide), 0, block)(right, left)
    kv_own = [first, second]
    kv_other = [swap(x, CORE) for x in kv_own]
    qg_all = exchange(qg, QUERY_GROUP).reshape(columns, 2 * wide)
    big = shape(F32, 2 * rows, columns)
    pairs = 2 * rows * columns
    stats_shape = shape(F32, QUERIES_IN, 8, columns // 2)
    w1, w2, dp, stats, tops = call(
        forward, (big, big, big, stats_shape, shape(F32, 2, columns)), 2 * pairs * wide * 9, 4 * pairs * 3
    )(*kv_own, *kv_other, qg_all)
    every = exchange(stats, QUERY_GROUP)
    half_out = (shape(F32, rows, 2 * wide), shape(BF16, 6, rows, columns))
    other, other_slopes = call(
        functools.partial(key_side, rows), half_out, pairs * wide * 6, 4 * pairs * 3
    )(w1, w2, dp, qg_all, tops, every)
    moved = swap(other, CORE)
    own, dq = call(
        functools.partial(own_half, 4),
        (shape(F32, rows, 2 * wide), shape(F32, columns, 2 * wide)),
        3 * pairs * wide * 6,
        4 * pairs * 4,
        scratch_shapes=[pltpu.VMEM((6, rows, columns), BF16), pltpu.VMEM((2, 2 * wide, 2 * rows), BF16)],
    )(*kv_own, *kv_other, w1, w2, dp, qg_all, tops, every, other_slopes)
    vmem, anywhere = pl.BlockSpec(memory_space=pltpu.VMEM), pl.BlockSpec(memory_space=pl.ANY)
    pair_sum, block_sum = shape(F32, NEAR * own_keys, 2 * wide), shape(F32, own_keys, 2 * wide)
    mine, far, right, left, left_past, dq = call(
        add_moved,
        (pair_sum,) * 3 + (block_sum,) * 2 + (shape(F32, columns, 2 * wide),),
        0,
        block,
        in_specs=[vmem, vmem, anywhere],
        out_specs=[vmem] * 5 + [anywhere],
        input_output_aliases={2: 5},
    )(own, moved, dq)
    dq_parts = exchange(dq.reshape(QUERIES_IN, own_rows, 2 * wide), QUERY_GROUP)
    sides = (toward(left, -1), past(left_past, -1))
    near, beyond = call(add_ring, (block_sum,) * NEAR, 10**9, block)(mine, across(far), toward(right, 1))
    grad_keys, grad_values, attended, grad_queries = call(
        finish, (shape(F32, own_keys, wide),) * 2 + (shape(F32, own_rows, wide),) * 2, 0, block
    )(near, *sides, swap(beyond, PAIR), dq_parts)
    return attended, grad_queries, grad_keys, grad_values


def solution(mesh):
    fine = Mesh(mesh.devices.reshape((2,) * 9), PB + KA)
    by_query, by_key = P(KA + PB, None), P(PB + KA, None)
    return jax.shard_map(
        per_device,
        mesh=fine,
        in_specs=(by_query, by_key, by_key, by_query),
        out_specs=(by_query, by_query, by_key, by_key),
        check_vma=False,
    )
```
